256 devices in a mesh: seq: 32 (over z_hi, y, core), head: 8 (over z_lo, x).
Axes of the slice: x: 4, y: 4, z: 8 (z_hi: 4, z_lo: 2; z = z_hi * 2 + z_lo), core: 2. Of those that a mesh axis runs over, the one named last changes fastest.
Arguments:
- tokens: bfloat16 [16384, 5120], P(('seq', 'head')), may hold values from -6 to 6
- w_qkv: bfloat16 [3, 5120, 2560], P(None, None, 'head'), may hold values from -0.078125 to 0.078125
- scale_exp: int32 [3, 40, 8], P(None, None, 'head'), may hold values from -2 to 1
- gate_mask: int32 [16384, 8], P('seq', 'head'), may hold values 0 or 1
- rate: float32 [8], P('head'), may hold values from 0.0003125 to 0.0015625
- fast_gate: bfloat16 [8, 320, 640], P('head'), may hold values from -0.3125 to 0.3125
- fast_up: bfloat16 [8, 320, 640], P('head'), may hold values from -0.3125 to 0.3125
- fast_down: bfloat16 [8, 320, 640], P('head'), may hold values from -0.25 to 0.25
Outputs:
- answers: bfloat16 [16384, 2560], P(('seq', 'head'))
The draws below stay inside these ranges and needn't reach their ends.
All inputs are finite; a program needn't handle non-finite values. No bound on the sum of `gate_mask` on one device may be relied on, other than what follows from the above.
Results may differ from the reference program's by a relative error of at most 0.012.
Values may be sent and summed in bfloat16 or wider, within the bound.
No kernel may reach another device: no remote copies, remote signals or barrier semaphores. Data moves between devices by JAX's collectives and lax.ppermute only.
A program may use at most 64 MiB of HBM per device.

```python
import math
import jax
import jax.numpy as jnp
from jax import lax

D = 5120
HD = 320
HID = 640
SB = 128
HEADS = 8
TOKENS = 16384


def plant(drawn, stream_key, least, top_value):
    longest = drawn.shape.index(max(drawn.shape))
    spots = []
    for shift in (0, 1):
        where = [jax.random.randint(jax.random.fold_in(stream_key, axis), (), 0, length) for axis, length in enumerate(drawn.shape)]
        where[longest] = (where[longest] + shift) % drawn.shape[longest]
        spots.append(tuple(where))
    return drawn.at[spots[0]].set(least).at[spots[1]].set(top_value)


def steps_of(rng, shape, shards, smallest, largest):
    loudness, own = 1.0, jax.random.fold_in(rng, 6)
    for axis_at, shards_of in shards:
        steps = jnp.exp(jax.random.uniform(jax.random.fold_in(own, axis_at), (shards_of,), jnp.float32, smallest / len(shards), largest / len(shards)))
        loudness = loudness * jnp.repeat(steps, shape[axis_at] // shards_of).reshape([-1 if axis == axis_at else 1 for axis in range(len(shape))])
    return loudness


def gaussian(key, shape, width, limit, cuts=(), kind=jnp.bfloat16):
    loudness = steps_of(key, shape, cuts, -0.22, 0.18) if cuts else 1.0
    values = jax.random.normal(key, shape, jnp.float32) * width * loudness
    return jnp.minimum(jnp.maximum(values, -limit), limit).astype(kind)


def setup_inputs(seed: int = 0) -> dict:
    streams_of = jax.random.split(jax.random.key(seed), 9)
    tokens = gaussian(streams_of[0], (TOKENS, D), 1.0, 6.0, ((0, 256),))
    w_qkv = gaussian(streams_of[1], (3, D, HEADS * HD), D ** -0.5, 0.078125, ((2, 8),))
    scale_exp = plant(jax.random.randint(streams_of[2], (3, D // SB, HEADS), -2, 2), jax.random.fold_in(streams_of[2], 1), -2, 1).astype(jnp.int32)
    gate_mask = plant((jax.random.randint(streams_of[3], (TOKENS, HEADS), 0, 2) < 1).astype(jnp.int32), jax.random.fold_in(streams_of[3], 1), 0, 1)
    rate = jnp.clip(jnp.exp(math.log(0.0015625) - 1.609438 * jax.random.uniform(streams_of[4], (HEADS,), jnp.float32) ** steps_of(streams_of[4], (HEADS,), ((0, 8),), -0.2, 0.2)), 0.0003125, 0.0015625)
    fast_gate = gaussian(streams_of[5], (HEADS, HD, HID), HD ** -0.5, 0.3125, ((0, 8),))
    fast_up = gaussian(streams_of[6], (HEADS, HD, HID), HD ** -0.5, 0.3125, ((0, 8),))
    fast_down = gaussian(streams_of[7], (HEADS, HD, HID), HID ** -0.5, 0.25, ((0, 8),))
    return dict(tokens=tokens, w_qkv=w_qkv, scale_exp=scale_exp, gate_mask=gate_mask, rate=rate, fast_gate=fast_gate, fast_up=fast_up, fast_down=fast_down)


def expanded(w_qkv, scale_exp):
    factor = jnp.exp2(scale_exp.astype(jnp.float32))
    factor = jnp.repeat(jnp.repeat(factor, SB, axis=1), HD, axis=2)
    return (w_qkv.astype(jnp.float32) * factor).astype(jnp.bfloat16)

def local_grads(keys, values, weight, old):
    gate = jnp.dot(keys, old[0], preferred_element_type=jnp.float32)
    upper = jnp.dot(keys, old[1], preferred_element_type=jnp.float32)
    sigma = jax.nn.sigmoid(gate)
    active = gate * sigma
    hidden = (active * upper).astype(jnp.bfloat16)
    weighted = (weight[:, None] * values.astype(jnp.float32)).astype(jnp.bfloat16)
    d_hidden = jnp.dot(weighted, old[2], preferred_element_type=jnp.float32)
    d_gate = (d_hidden * upper * sigma * (1.0 + gate * (1.0 - sigma))).astype(jnp.bfloat16)
    d_upper = (d_hidden * active).astype(jnp.bfloat16)
    dims = (((0,), (0,)), ((), ()))
    grad_gate = lax.dot_general(keys, d_gate, dims, preferred_element_type=jnp.float32)
    grad_upper = lax.dot_general(keys, d_upper, dims, preferred_element_type=jnp.float32)
    grad_down = lax.dot_general(weighted, hidden, dims, preferred_element_type=jnp.float32)
    return jnp.stack([grad_gate, grad_upper, grad_down])

def respond(query, renorm):
    gate = jnp.dot(query, renorm[0], preferred_element_type=jnp.float32)
    upper = jnp.dot(query, renorm[1], preferred_element_type=jnp.float32)
    hidden = (jax.nn.silu(gate) * upper).astype(jnp.bfloat16)
    output = lax.dot_general(hidden, renorm[2], (((1,), (1,)), ((), ())), preferred_element_type=jnp.float32)
    scaled = output * lax.rsqrt(lax.optimization_barrier(jnp.mean(output * output, axis=-1, keepdims=True)) + 1e-05)
    return scaled.astype(jnp.bfloat16)

def reference(tokens, w_qkv, scale_exp, gate_mask, rate, fast_gate, fast_up, fast_down):
    weff = expanded(w_qkv, scale_exp)
    projected = [jnp.dot(tokens, weff[c], preferred_element_type=jnp.float32).astype(jnp.bfloat16) for c in range(3)]
    split = [p.reshape(TOKENS, HEADS, HD).transpose(1, 0, 2) for p in projected]
    masks = gate_mask.astype(jnp.float32).T

    def one_head(items):
        query, keys, values, mask_row, head_rate, w_gate, w_up, w_down = items
        old = jnp.stack([w_gate, w_up, w_down])
        grads = local_grads(keys, values, head_rate * mask_row, old)
        old_f = old.astype(jnp.float32)
        old_norm = jnp.sqrt(lax.optimization_barrier(jnp.sum(old_f * old_f, axis=1)))
        fresh = old_f + grads
        new_sq = lax.optimization_barrier(jnp.sum(fresh * fresh, axis=1))
        renorm = (fresh * (old_norm / jnp.sqrt(new_sq + 1e-06))[:, None, :]).astype(jnp.bfloat16)
        return respond(query, renorm)
    result = lax.map(one_head, (split[0], split[1], split[2], masks, rate, fast_gate, fast_up, fast_down))
    return result.transpose(1, 0, 2).reshape(TOKENS, HEADS * HD)
```

```python
import jax
import jax.numpy as jnp
from jax import lax
from jax.sharding import PartitionSpec as P

AXES = ("seq", "head")
BF16 = jnp.bfloat16
F32 = jnp.float32


def place(i):
    seq, head = divmod(i, 8)
    return seq // 8, (seq // 2) % 4, seq % 2, head // 4, head % 4


def permute(value, move):
    pairs = []
    for i in range(256):
        z_hi, y, core, z_lo, x = move(*place(i))
        pairs.append((i, ((z_hi % 4) * 8 + (y % 4) * 2 + core) * 8 + z_lo * 4 + x % 4))
    return lax.ppermute(value, AXES, pairs)


def to_core(value):
    return permute(value, lambda h, y, c, l, x: (h, y, 1 - c, l, x))


def to_y(value, d):
    return permute(value, lambda h, y, c, l, x: (h, y + d, c, l, x))


def to_z(value, d):
    return permute(value, lambda h, y, c, l, x: (h + d, y, c, l, x))


def local_grads(keys, values, weight, old):
    gate = jnp.dot(keys, old[0], preferred_element_type=F32)
    upper = jnp.dot(keys, old[1], preferred_element_type=F32)
    sigma = jax.nn.sigmoid(gate)
    active = gate * sigma
    hidden = (active * upper).astype(BF16)
    weighted = (weight[:, None] * values.astype(F32)).astype(BF16)
    d_hidden = jnp.dot(weighted, old[2], preferred_element_type=F32)
    d_gate = (d_hidden * upper * sigma * (1.0 + gate * (1.0 - sigma))).astype(BF16)
    d_upper = (d_hidden * active).astype(BF16)
    dims = (((0,), (0,)), ((), ()))
    return jnp.concatenate(
        [
            lax.dot_general(d_gate, keys, dims, preferred_element_type=F32),
            lax.dot_general(d_upper, keys, dims, preferred_element_type=F32),
            lax.dot_general(hidden, weighted, dims, preferred_element_type=F32),
        ],
        axis=1,
    )


def respond(query, renorm):
    dims = (((1,), (1,)), ((), ()))
    gate = lax.dot_general(query, renorm[:, :320], dims, preferred_element_type=F32)
    upper = lax.dot_general(query, renorm[:, 320:640], dims, preferred_element_type=F32)
    hidden = (jax.nn.silu(gate) * upper).astype(BF16)
    output = jnp.dot(hidden, renorm[:, 640:], preferred_element_type=F32)
    scaled = output * lax.rsqrt(jnp.mean(output * output, axis=-1, keepdims=True) + 1e-05)
    return scaled.astype(BF16)


def rows(value, start, size):
    return lax.dynamic_slice_in_dim(value, start, size, axis=0)


def body(tokens, w_qkv, scale_exp, gate_mask, rate, fast_gate, fast_up, fast_down):
    seq = lax.axis_index("seq")
    core, y = seq % 2, (seq // 2) % 4
    factor = jnp.exp2(scale_exp.astype(F32))[:, :, 0]
    block_rows = w_qkv.shape[1] // factor.shape[1]
    factor = jnp.repeat(factor, block_rows, axis=1)[:, :, None].astype(BF16)
    weff = w_qkv * factor
    triple = jnp.einsum(
        "rd,cdh->rch",
        lax.all_gather(tokens, "head", axis=0, tiled=True),
        weff,
        preferred_element_type=F32,
    ).astype(BF16)
    query, keys, values = triple[:, 0], triple[:, 1], triple[:, 2]
    weight = rate[0] * gate_mask[:, 0].astype(F32)
    old = jnp.stack([fast_gate[0], fast_up[0], fast_down[0]])
    part = local_grads(keys, values, weight, old)

    half = rows(part, core * 320, 320) + to_core(
        rows(part, (1 - core) * 320, 320).astype(BF16)
    ).astype(F32)
    piece = rows(half, y * 80, 80)
    for d in (1, 3, 2):
        piece += to_y(rows(half, (y + d) % 4 * 80, 80).astype(BF16), d).astype(F32)
    small = piece.astype(BF16)
    for d in (1, 3, 2):
        piece += to_z(small, d).astype(F32)

    old_t = jnp.concatenate([fast_gate[0].T, fast_up[0].T, fast_down[0].T], axis=1)
    old_f = rows(old_t, core * 320 + y * 80, 80).astype(F32).reshape(80, 3, 320)
    fresh = old_f + piece.reshape(80, 3, 320)
    old_norm = jnp.sqrt(jnp.sum(old_f * old_f, axis=2, keepdims=True))
    new_sq = jnp.sum(fresh * fresh, axis=2, keepdims=True)
    mine = (fresh * (old_norm / jnp.sqrt(new_sq + 1e-06))).astype(BF16).reshape(80, 960)
    column = jnp.concatenate([mine, to_y(mine, 1), to_y(mine, 3), to_y(mine, 2)], axis=0)
    renorm = jnp.concatenate([column, to_core(column)], axis=0)

    answer = respond(query, renorm)
    return lax.all_to_all(answer, "head", split_axis=0, concat_axis=1, tiled=True)


def solution(mesh):
    in_specs = (
        P(("seq", "head"), None),
        P(None, None, "head"),
        P(None, None, "head"),
        P("seq", "head"),
        P("head"),
        P("head", None, None),
        P("head", None, None),
        P("head", None, None),
    )
    out_specs = P(("seq", "head"), None)
    return jax.shard_map(body, mesh=mesh, in_specs=in_specs, out_specs=out_specs, check_vma=False)
```

```python
import jax
import jax.numpy as jnp
from jax import lax
from jax.sharding import PartitionSpec as P

AXES = ("seq", "head")
BF16 = jnp.bfloat16
F32 = jnp.float32


def place(i):
    seq, head = divmod(i, 8)
    return seq // 8, (seq // 2) % 4, seq % 2, head // 4, head % 4


def permute(value, move):
    pairs = []
    for i in range(256):
        z_hi, y, core, z_lo, x = move(*place(i))
        pairs.append((i, ((z_hi % 4) * 8 + (y % 4) * 2 + core) * 8 + z_lo * 4 + x % 4))
    return lax.ppermute(value, AXES, pairs)


def to_core(value):
    return permute(value, lambda h, y, c, l, x: (h, y, 1 - c, l, x))


def to_y(value, d):
    return permute(value, lambda h, y, c, l, x: (h, y + d, c, l, x))


def to_z(value, d):
    return permute(value, lambda h, y, c, l, x: (h + d, y, c, l, x))


def near(x):
    return x ^ 1


def far(x):
    return (x + 1) % 4 if x % 2 else (x - 1) % 4


def to_near_x(value):
    return permute(value, lambda h, y, c, l, x: (h, y, c, l, near(x)))


def to_far_x(value):
    return permute(value, lambda h, y, c, l, x: (h, y, c, l, far(x)))


def to_opposite_x(value):
    return permute(value, lambda h, y, c, l, x: (h, y, c, l, x + 2))


def to_near_z(value):
    return permute(value, lambda h, y, c, l, x: (h, y, c, 1 - l, x))


def to_far_z(value):
    return permute(value, lambda h, y, c, l, x: (h + 1 if l else h - 1, y, c, 1 - l, x))


def local_grads(keys, values, weight, old):
    gate = jnp.dot(keys, old[0], preferred_element_type=F32)
    upper = jnp.dot(keys, old[1], preferred_element_type=F32)
    sigma = jax.nn.sigmoid(gate)
    active = gate * sigma
    hidden = (active * upper).astype(BF16)
    weighted = (weight[:, None] * values.astype(F32)).astype(BF16)
    d_hidden = jnp.dot(weighted, old[2], preferred_element_type=F32)
    d_gate = (d_hidden * upper * sigma * (1.0 + gate * (1.0 - sigma))).astype(BF16)
    d_upper = (d_hidden * active).astype(BF16)
    dims = (((0,), (0,)), ((), ()))
    return jnp.concatenate(
        [
            lax.dot_general(d_gate, keys, dims, preferred_element_type=F32),
            lax.dot_general(d_upper, keys, dims, preferred_element_type=F32),
            lax.dot_general(hidden, weighted, dims, preferred_element_type=F32),
        ],
        axis=1,
    )


def respond(query, renorm):
    dims = (((1,), (1,)), ((), ()))
    gate = lax.dot_general(query, renorm[:, :320], dims, preferred_element_type=F32)
    upper = lax.dot_general(query, renorm[:, 320:640], dims, preferred_element_type=F32)
    hidden = (jax.nn.silu(gate) * upper).astype(BF16)
    output = jnp.dot(hidden, renorm[:, 640:], preferred_element_type=F32)
    scaled = output * lax.rsqrt(jnp.mean(output * output, axis=-1, keepdims=True) + 1e-05)
    return scaled.astype(BF16)


def rows(value, start, size):
    return lax.dynamic_slice_in_dim(value, start, size, axis=0)


def gather(tokens):
    first, second = tokens[:32], tokens[32:]
    near_tile, far_tile = to_near_x(tokens), to_far_x(tokens)
    z1, z2 = to_near_z(first), to_far_z(second)
    opposite_first = to_far_x(near_tile[:32])
    opposite_second = to_near_x(far_tile[32:])
    z3 = to_near_z(jnp.concatenate([near_tile[:32], far_tile[:32]]))
    z4 = to_far_z(jnp.concatenate([near_tile[32:], far_tile[32:]]))
    z5, z6 = to_near_z(opposite_first), to_far_z(opposite_second)
    return (
        jnp.concatenate([tokens, near_tile, far_tile, opposite_first, opposite_second]),
        jnp.concatenate([z1, z3, z5, z2, z4, z6]),
    )


def x_order(x):
    return [x, x ^ 1, (x + jnp.where(x % 2 == 1, 1, 3)) % 4, (x + 2) % 4]


def weights_of_rows(weight, z_lo, x):
    tiles = weight.reshape(8, 64)
    same = lax.dynamic_slice_in_dim(tiles, z_lo * 4, 4, axis=0)
    other = lax.dynamic_slice_in_dim(tiles, (1 - z_lo) * 4, 4, axis=0)
    order = x_order(x)
    pick = lambda t: jnp.concatenate([lax.dynamic_slice_in_dim(t, i, 1, axis=0) for i in order])
    same, other = pick(same), pick(other)
    moved = permute(other[:, 32:], lambda h, y, c, l, x: (h - 1 if l else h + 1, y, c, l, x))
    return jnp.concatenate([same.reshape(256), other[:, :32].reshape(128), moved.reshape(128)])


def send_back(answer, z_lo, x):
    from_near = to_near_z(answer[256:384]).reshape(4, 32, 320)
    from_far = to_far_z(answer[384:]).reshape(4, 32, 320)
    other = jnp.concatenate([from_near, from_far], axis=1)
    both = jnp.stack([answer[:256].reshape(4, 64, 320), other], axis=1)
    slots = jnp.stack(
        [both[0], to_near_x(both[1]), to_far_x(both[2]), to_opposite_x(both[3])]
    ).reshape(8, 64, 320)
    out = []
    for head in range(8):
        d = (head % 4 - x) % 4
        at = jnp.where(d == 0, 0, jnp.where(d == 2, 3, jnp.where(head % 4 == x ^ 1, 1, 2)))
        slot = at * 2 + jnp.where(head // 4 == z_lo, 0, 1)
        out.append(lax.dynamic_slice_in_dim(slots, slot, 1, axis=0)[0])
    return jnp.concatenate(out, axis=1)


def body(tokens, w_qkv, scale_exp, gate_mask, rate, fast_gate, fast_up, fast_down):
    seq, head = lax.axis_index("seq"), lax.axis_index("head")
    core, y = seq % 2, (seq // 2) % 4
    z_lo, x = head // 4, head % 4
    factor = jnp.exp2(scale_exp.astype(F32))[:, :, 0]
    block_rows = w_qkv.shape[1] // factor.shape[1]
    factor = jnp.repeat(factor, block_rows, axis=1)[:, :, None].astype(BF16)
    weff = lax.optimization_barrier(w_qkv * factor)
    weight = weights_of_rows(rate[0] * gate_mask[:, 0].astype(F32), z_lo, x)
    plane, others = gather(tokens)
    def project(tile, c):
        return jnp.dot(tile, weff[c], preferred_element_type=F32).astype(BF16)
    keys = jnp.concatenate([project(plane, 1), project(others, 1)])
    values = jnp.concatenate([project(plane, 2), project(others, 2)])
    query = jnp.concatenate([project(plane, 0), project(others, 0)])
    old = jnp.stack([fast_gate[0], fast_up[0], fast_down[0]])
    part = local_grads(keys, values, weight, old)

    half = rows(part, core * 320, 320) + to_core(
        rows(part, (1 - core) * 320, 320).astype(BF16)
    ).astype(F32)
    piece = rows(half, y * 80, 80)
    for d in (1, 3, 2):
        piece += to_y(rows(half, (y + d) % 4 * 80, 80).astype(BF16), d).astype(F32)
    small = piece.astype(BF16)
    for d in (1, 3, 2):
        piece += to_z(small, d).astype(F32)

    old_t = jnp.concatenate([fast_gate[0].T, fast_up[0].T, fast_down[0].T], axis=1)
    old_f = rows(old_t, core * 320 + y * 80, 80).astype(F32).reshape(80, 3, 320)
    fresh = old_f + piece.reshape(80, 3, 320)
    old_norm = jnp.sqrt(jnp.sum(old_f * old_f, axis=2, keepdims=True))
    new_sq = jnp.sum(fresh * fresh, axis=2, keepdims=True)
    mine = (fresh * (old_norm / jnp.sqrt(new_sq + 1e-06))).astype(BF16).reshape(80, 960)
    column = jnp.concatenate([mine, to_y(mine, 1), to_y(mine, 3), to_y(mine, 2)], axis=0)
    renorm = jnp.concatenate([column, to_core(column)], axis=0)

    answer = respond(query, renorm)
    return send_back(answer, z_lo, x)


def solution(mesh):
    in_specs = (
        P(("seq", "head"), None),
        P(None, None, "head"),
        P(None, None, "head"),
        P("seq", "head"),
        P("head"),
        P("head", None, None),
        P("head", None, None),
        P("head", None, None),
    )
    out_specs = P(("seq", "head"), None)
    return jax.shard_map(body, mesh=mesh, in_specs=in_specs, out_specs=out_specs, check_vma=False)
```

```python
import jax
import jax.numpy as jnp
from jax import lax
from jax.sharding import PartitionSpec as P

AXES = ("seq", "head")
BF16 = jnp.bfloat16
F32 = jnp.float32


def place(i):
    seq, head = divmod(i, 8)
    return seq // 8, (seq // 2) % 4, seq % 2, head // 4, head % 4


def permute(value, move):
    pairs = []
    for i in range(256):
        z_hi, y, core, z_lo, x = move(*place(i))
        pairs.append((i, ((z_hi % 4) * 8 + (y % 4) * 2 + core) * 8 + z_lo * 4 + x % 4))
    return lax.ppermute(value, AXES, pairs)


def to_core(value):
    return permute(value, lambda h, y, c, l, x: (h, y, 1 - c, l, x))


def to_y(value, d):
    return permute(value, lambda h, y, c, l, x: (h, y + d, c, l, x))


def to_near_h(value):
    return permute(value, lambda h, y, c, l, x: (near(h), y, c, l, x))


def to_far_h(value):
    return permute(value, lambda h, y, c, l, x: (far(h), y, c, l, x))


def near(x):
    return x ^ 1


def far(x):
    return (x + 1) % 4 if x % 2 else (x - 1) % 4


def to_near_x(value):
    return permute(value, lambda h, y, c, l, x: (h, y, c, l, near(x)))


def to_far_x(value):
    return permute(value, lambda h, y, c, l, x: (h, y, c, l, far(x)))


def to_opposite_x(value):
    return permute(value, lambda h, y, c, l, x: (h, y, c, l, x + 2))


def to_near_z(value):
    return permute(value, lambda h, y, c, l, x: (h, y, c, 1 - l, x))


def to_far_z(value):
    return permute(value, lambda h, y, c, l, x: (h + 1 if l else h - 1, y, c, 1 - l, x))


def local_grads(keys, values, weight, old):
    gate = jnp.dot(keys, old[0], preferred_element_type=F32)
    upper = jnp.dot(keys, old[1], preferred_element_type=F32)
    sigma = jax.nn.sigmoid(gate)
    active = gate * sigma
    hidden = (active * upper).astype(BF16)
    weighted = (weight[:, None] * values.astype(F32)).astype(BF16)
    d_hidden = jnp.dot(weighted, old[2], preferred_element_type=F32)
    d_gate = (d_hidden * upper * sigma * (1.0 + gate * (1.0 - sigma))).astype(BF16)
    d_upper = (d_hidden * active).astype(BF16)
    dims = (((0,), (0,)), ((), ()))
    return jnp.concatenate(
        [
            lax.dot_general(d_gate, keys, dims, preferred_element_type=F32),
            lax.dot_general(d_upper, keys, dims, preferred_element_type=F32),
            lax.dot_general(hidden, weighted, dims, preferred_element_type=F32),
        ],
        axis=1,
    )


def respond(query, renorm):
    dims = (((1,), (1,)), ((), ()))
    gate = lax.dot_general(query, renorm[:, :320], dims, preferred_element_type=F32)
    upper = lax.dot_general(query, renorm[:, 320:640], dims, preferred_element_type=F32)
    hidden = (jax.nn.silu(gate) * upper).astype(BF16)
    output = jnp.dot(hidden, renorm[:, 640:], preferred_element_type=F32)
    scaled = output * lax.rsqrt(jnp.mean(output * output, axis=-1, keepdims=True) + 1e-05)
    return scaled.astype(BF16)


def rows(value, start, size):
    return lax.dynamic_slice_in_dim(value, start, size, axis=0)


def gather(tokens):
    first, second = tokens[:32], tokens[32:]
    near_tile, far_tile = to_near_x(tokens), to_far_x(tokens)
    z1, z2 = to_near_z(first), to_far_z(second)
    opposite_first = to_far_x(near_tile[:32])
    opposite_second = to_near_x(far_tile[32:])
    z3 = to_near_z(jnp.concatenate([near_tile[:32], far_tile[:32]]))
    z4 = to_far_z(jnp.concatenate([near_tile[32:], far_tile[32:]]))
    z5, z6 = to_near_z(opposite_first), to_far_z(opposite_second)
    return (
        jnp.concatenate([tokens, near_tile, far_tile]),
        jnp.concatenate([opposite_first, opposite_second, z1, z3, z2, z4]),
        jnp.concatenate([z5, z6]),
    )


def x_order(x):
    return [x, x ^ 1, (x + jnp.where(x % 2 == 1, 1, 3)) % 4, (x + 2) % 4]


def weights_of_rows(weight, z_lo, x):
    tiles = weight.reshape(8, 64)
    same = lax.dynamic_slice_in_dim(tiles, z_lo * 4, 4, axis=0)
    other = lax.dynamic_slice_in_dim(tiles, (1 - z_lo) * 4, 4, axis=0)
    order = x_order(x)
    pick = lambda t: jnp.concatenate([lax.dynamic_slice_in_dim(t, i, 1, axis=0) for i in order])
    same, other = pick(same), pick(other)
    moved = permute(other[:, 32:], lambda h, y, c, l, x: (h - 1 if l else h + 1, y, c, l, x))
    other = other[:, :32]
    return jnp.concatenate(
        [same.reshape(256), other[:3].reshape(96), moved[:3].reshape(96), other[3], moved[3]]
    )


def send_back(plane, others, z_lo, x):
    from_near = to_near_z(jnp.concatenate([others[:96], others[192:224]])).reshape(4, 32, 320)
    from_far = to_far_z(jnp.concatenate([others[96:192], others[224:]])).reshape(4, 32, 320)
    other = jnp.concatenate([from_near, from_far], axis=1)
    both = jnp.stack([plane.reshape(4, 64, 320), other], axis=1)
    slots = jnp.stack(
        [both[0], to_near_x(both[1]), to_far_x(both[2]), to_opposite_x(both[3])]
    ).reshape(8, 64, 320)
    out = []
    for head in range(8):
        d = (head % 4 - x) % 4
        at = jnp.where(d == 0, 0, jnp.where(d == 2, 3, jnp.where(head % 4 == x ^ 1, 1, 2)))
        slot = at * 2 + jnp.where(head // 4 == z_lo, 0, 1)
        out.append(lax.dynamic_slice_in_dim(slots, slot, 1, axis=0)[0])
    return jnp.concatenate(out, axis=1)


def body(tokens, w_qkv, scale_exp, gate_mask, rate, fast_gate, fast_up, fast_down):
    seq, head = lax.axis_index("seq"), lax.axis_index("head")
    core, y = seq % 2, (seq // 2) % 4
    z_lo, x = head // 4, head % 4
    factor = jnp.exp2(scale_exp.astype(F32))[:, :, 0]
    block_rows = w_qkv.shape[1] // factor.shape[1]
    factor = jnp.repeat(factor, block_rows, axis=1)[:, :, None].astype(BF16)
    weff_kv = lax.optimization_barrier(w_qkv[1:] * factor[1:])
    weight = weights_of_rows(rate[0] * gate_mask[:, 0].astype(F32), z_lo, x)
    batches = gather(tokens)

    def project(tiles, w):
        return jnp.concatenate([jnp.dot(t, w, preferred_element_type=F32).astype(BF16) for t in tiles])

    keys, values = project(batches, weff_kv[0]), project(batches, weff_kv[1])
    old = jnp.stack([fast_gate[0], fast_up[0], fast_down[0]])
    part = local_grads(keys, values, weight, old)

    half = rows(part, core * 320, 320) + to_core(
        rows(part, (1 - core) * 320, 320).astype(BF16)
    ).astype(F32)
    piece = rows(half, y * 80, 80)
    for d in (1, 3, 2):
        piece += to_y(rows(half, (y + d) % 4 * 80, 80).astype(BF16), d).astype(F32)
    weff_q = w_qkv[0] * factor[0]
    upper, lower = piece[:40], piece[40:]
    batches, upper, lower = lax.optimization_barrier((batches, upper, lower))
    got = to_near_h(upper.astype(BF16)), to_far_h(lower.astype(BF16))
    query_a = project(batches[:1], weff_q)
    query_a, got = lax.optimization_barrier((query_a, got))
    upper, lower = upper + got[0].astype(F32), lower + got[1].astype(F32)
    batches, upper, lower = lax.optimization_barrier((batches, upper, lower))
    got = to_far_h(upper.astype(BF16)), to_near_h(lower.astype(BF16))
    query_b = project(batches[1:], weff_q)
    query_b, got = lax.optimization_barrier((query_b, got))
    piece = jnp.concatenate([upper + got[0].astype(F32), lower + got[1].astype(F32)])
    query = jnp.concatenate([query_a, query_b])

    old_t = jnp.concatenate([fast_gate[0].T, fast_up[0].T, fast_down[0].T], axis=1)
    old_f = rows(old_t, core * 320 + y * 80, 80).astype(F32).reshape(80, 3, 320)
    fresh = old_f + piece.reshape(80, 3, 320)
    old_norm = jnp.sqrt(jnp.sum(old_f * old_f, axis=2, keepdims=True))
    new_sq = jnp.sum(fresh * fresh, axis=2, keepdims=True)
    mine = (fresh * (old_norm / jnp.sqrt(new_sq + 1e-06))).astype(BF16).reshape(80, 960)
    column = jnp.concatenate([mine, to_y(mine, 1), to_y(mine, 3), to_y(mine, 2)], axis=0)
    renorm = jnp.concatenate([column, to_core(column)], axis=0)

    others = respond(query[256:], renorm)
    plane = respond(query[:256], renorm)
    return send_back(plane, others, z_lo, x)


def solution(mesh):
    in_specs = (
        P(("seq", "head"), None),
        P(None, None, "head"),
        P(None, None, "head"),
        P("seq", "head"),
        P("head"),
        P("head", None, None),
        P("head", None, None),
        P("head", None, None),
    )
    out_specs = P(("seq", "head"), None)
    return jax.shard_map(body, mesh=mesh, in_specs=in_specs, out_specs=out_specs, check_vma=False)
```

```python
import jax
import jax.numpy as jnp
from jax import lax
from jax.sharding import PartitionSpec as P

AXES = ("seq", "head")
BF16 = jnp.bfloat16
F32 = jnp.float32


def place(i):
    seq, head = divmod(i, 8)
    return seq // 8, (seq // 2) % 4, seq % 2, head // 4, head % 4


def permute(value, move):
    pairs = []
    for i in range(256):
        z_hi, y, core, z_lo, x = move(*place(i))
        pairs.append((i, ((z_hi % 4) * 8 + (y % 4) * 2 + core) * 8 + z_lo * 4 + x % 4))
    return lax.ppermute(value, AXES, pairs)


def to_core(value):
    return permute(value, lambda h, y, c, l, x: (h, y, 1 - c, l, x))


def to_y(value, d):
    return permute(value, lambda h, y, c, l, x: (h, y + d, c, l, x))


def to_z(value, d):
    return permute(value, lambda h, y, c, l, x: (h + d, y, c, l, x))


def near(x):
    return x ^ 1


def far(x):
    return (x + 1) % 4 if x % 2 else (x - 1) % 4


def to_near_x(value):
    return permute(value, lambda h, y, c, l, x: (h, y, c, l, near(x)))


def to_far_x(value):
    return permute(value, lambda h, y, c, l, x: (h, y, c, l, far(x)))


def to_opposite_x(value):
    return permute(value, lambda h, y, c, l, x: (h, y, c, l, x + 2))


def to_near_z(value):
    return permute(value, lambda h, y, c, l, x: (h, y, c, 1 - l, x))


def to_far_z(value):
    return permute(value, lambda h, y, c, l, x: (h + 1 if l else h - 1, y, c, 1 - l, x))


def local_grads(keys, values, weight, old):
    gate = jnp.dot(keys, old[0], preferred_element_type=F32)
    upper = jnp.dot(keys, old[1], preferred_element_type=F32)
    sigma = jax.nn.sigmoid(gate)
    active = gate * sigma
    hidden = (active * upper).astype(BF16)
    weighted = (weight[:, None] * values.astype(F32)).astype(BF16)
    d_hidden = jnp.dot(weighted, old[2], preferred_element_type=F32)
    d_gate = (d_hidden * upper * sigma * (1.0 + gate * (1.0 - sigma))).astype(BF16)
    d_upper = (d_hidden * active).astype(BF16)
    dims = (((0,), (0,)), ((), ()))
    return jnp.concatenate(
        [
            lax.dot_general(d_gate, keys, dims, preferred_element_type=F32),
            lax.dot_general(d_upper, keys, dims, preferred_element_type=F32),
            lax.dot_general(hidden, weighted, dims, preferred_element_type=F32),
        ],
        axis=1,
    )


def respond(query, renorm):
    dims = (((1,), (1,)), ((), ()))
    gate = lax.dot_general(query, renorm[:, :320], dims, preferred_element_type=F32)
    upper = lax.dot_general(query, renorm[:, 320:640], dims, preferred_element_type=F32)
    hidden = (jax.nn.silu(gate) * upper).astype(BF16)
    output = jnp.dot(hidden, renorm[:, 640:], preferred_element_type=F32)
    scaled = output * lax.rsqrt(jnp.mean(output * output, axis=-1, keepdims=True) + 1e-05)
    return scaled.astype(BF16)


def rows(value, start, size):
    return lax.dynamic_slice_in_dim(value, start, size, axis=0)


def gather(tokens):
    first, second = tokens[:32], tokens[32:]
    near_tile, far_tile = to_near_x(tokens), to_far_x(tokens)
    z1, z2 = to_near_z(first), to_far_z(second)
    opposite_first = to_far_x(near_tile[:32])
    opposite_second = to_near_x(far_tile[32:])
    z3 = to_near_z(jnp.concatenate([near_tile[:32], far_tile[:32]]))
    z4 = to_far_z(jnp.concatenate([near_tile[32:], far_tile[32:]]))
    z5, z6 = to_near_z(opposite_first), to_far_z(opposite_second)
    return (
        [tokens, near_tile, far_tile, opposite_first, opposite_second],
        [z1, z3, z5, z2, z4, z6],
    )


def x_order(x):
    return [x, x ^ 1, (x + jnp.where(x % 2 == 1, 1, 3)) % 4, (x + 2) % 4]


def weights_of_rows(weight, z_lo, x):
    tiles = weight.reshape(8, 64)
    same = lax.dynamic_slice_in_dim(tiles, z_lo * 4, 4, axis=0)
    other = lax.dynamic_slice_in_dim(tiles, (1 - z_lo) * 4, 4, axis=0)
    order = x_order(x)
    pick = lambda t: jnp.concatenate([lax.dynamic_slice_in_dim(t, i, 1, axis=0) for i in order])
    same, other = pick(same), pick(other)
    moved = permute(other[:, 32:], lambda h, y, c, l, x: (h - 1 if l else h + 1, y, c, l, x))
    return jnp.concatenate([same.reshape(256), other[:, :32].reshape(128), moved.reshape(128)])


def send_back(plane, others, z_lo, x):
    from_near = to_near_z(others[:128]).reshape(4, 32, 320)
    from_far = to_far_z(others[128:]).reshape(4, 32, 320)
    other = jnp.concatenate([from_near, from_far], axis=1)
    both = jnp.stack([plane.reshape(4, 64, 320), other], axis=1)
    slots = jnp.stack(
        [both[0], to_near_x(both[1]), to_far_x(both[2]), to_opposite_x(both[3])]
    ).reshape(8, 64, 320)
    out = []
    for head in range(8):
        d = (head % 4 - x) % 4
        at = jnp.where(d == 0, 0, jnp.where(d == 2, 3, jnp.where(head % 4 == x ^ 1, 1, 2)))
        slot = at * 2 + jnp.where(head // 4 == z_lo, 0, 1)
        out.append(lax.dynamic_slice_in_dim(slots, slot, 1, axis=0)[0])
    return jnp.concatenate(out, axis=1)


def body(tokens, w_qkv, scale_exp, gate_mask, rate, fast_gate, fast_up, fast_down):
    seq, head = lax.axis_index("seq"), lax.axis_index("head")
    core, y = seq % 2, (seq // 2) % 4
    z_lo, x = head // 4, head % 4
    factor = jnp.exp2(scale_exp.astype(F32))[:, :, 0]
    block_rows = w_qkv.shape[1] // factor.shape[1]
    factor = jnp.repeat(factor, block_rows, axis=1)[:, :, None].astype(BF16)
    weff_kv = lax.optimization_barrier(w_qkv[1:] * factor[1:])
    weight = weights_of_rows(rate[0] * gate_mask[:, 0].astype(F32), z_lo, x)
    plane, others = gather(tokens)

    def project(tile, w):
        return jnp.dot(tile, w, preferred_element_type=F32).astype(BF16)

    plane, others[1], others[4] = lax.optimization_barrier((plane, others[1], others[4]))
    plane = jnp.concatenate(plane)
    weff_q = w_qkv[0] * factor[0]
    ready = project(plane, weff_kv[0]), project(plane, weff_kv[1]), project(plane, weff_q)
    ready, others = lax.optimization_barrier((ready, others))
    others = jnp.concatenate(others)
    keys = jnp.concatenate([ready[0], project(others, weff_kv[0])])
    values = jnp.concatenate([ready[1], project(others, weff_kv[1])])
    old = jnp.stack([fast_gate[0], fast_up[0], fast_down[0]])
    part = local_grads(keys, values, weight, old)

    half = rows(part, core * 320, 320) + to_core(
        rows(part, (1 - core) * 320, 320).astype(BF16)
    ).astype(F32)
    piece = rows(half, y * 80, 80)
    for d in (1, 3, 2):
        piece += to_y(rows(half, (y + d) % 4 * 80, 80).astype(BF16), d).astype(F32)
    others, piece = lax.optimization_barrier((others, piece))
    small = piece.astype(BF16)
    got = to_z(small, 2), to_z(small, 1), to_z(small, 3)
    query_others, got = lax.optimization_barrier((project(others, weff_q), got))
    for term in got:
        piece += term.astype(F32)

    old_t = jnp.concatenate([fast_gate[0].T, fast_up[0].T, fast_down[0].T], axis=1)
    old_f = rows(old_t, core * 320 + y * 80, 80).astype(F32).reshape(80, 3, 320)
    fresh = old_f + piece.reshape(80, 3, 320)
    old_norm = jnp.sqrt(jnp.sum(old_f * old_f, axis=2, keepdims=True))
    new_sq = jnp.sum(fresh * fresh, axis=2, keepdims=True)
    mine = (fresh * (old_norm / jnp.sqrt(new_sq + 1e-06))).astype(BF16).reshape(80, 960)
    column = jnp.concatenate([mine, to_y(mine, 1), to_y(mine, 3), to_y(mine, 2)], axis=0)
    renorm = jnp.concatenate([column, to_core(column)], axis=0)

    answers = respond(query_others, renorm)
    query_plane, answers = lax.optimization_barrier((ready[2], answers))
    return send_back(respond(query_plane, renorm), answers, z_lo, x)


def solution(mesh):
    in_specs = (
        P(("seq", "head"), None),
        P(None, None, "head"),
        P(None, None, "head"),
        P("seq", "head"),
        P("head"),
        P("head", None, None),
        P("head", None, None),
        P("head", None, None),
    )
    out_specs = P(("seq", "head"), None)
    return jax.shard_map(body, mesh=mesh, in_specs=in_specs, out_specs=out_specs, check_vma=False)
```

```python
import functools

import jax
import jax.numpy as jnp
from jax import lax
from jax.experimental import pallas as pl
from jax.experimental.pallas import tpu as pltpu
from jax.sharding import PartitionSpec as P

AXES = ("seq", "head")
BF16 = jnp.bfloat16
F32 = jnp.float32


def place(i):
    seq, head = divmod(i, 8)
    return seq // 8, (seq // 2) % 4, seq % 2, head // 4, head % 4


def permute(value, move):
    pairs = []
    for i in range(256):
        z_hi, y, core, z_lo, x = move(*place(i))
        pairs.append((i, ((z_hi % 4) * 8 + (y % 4) * 2 + core) * 8 + z_lo * 4 + x % 4))
    return lax.ppermute(value, AXES, pairs)


def to_core(value):
    return permute(value, lambda h, y, c, l, x: (h, y, 1 - c, l, x))


def to_y(value, d):
    return permute(value, lambda h, y, c, l, x: (h, y + d, c, l, x))


def to_z(value, d):
    return permute(value, lambda h, y, c, l, x: (h + d, y, c, l, x))


def near(x):
    return x ^ 1


def far(x):
    return (x + 1) % 4 if x % 2 else (x - 1) % 4


def to_near_x(value):
    return permute(value, lambda h, y, c, l, x: (h, y, c, l, near(x)))


def to_far_x(value):
    return permute(value, lambda h, y, c, l, x: (h, y, c, l, far(x)))


def to_opposite_x(value):
    return permute(value, lambda h, y, c, l, x: (h, y, c, l, x + 2))


def to_near_z(value):
    return permute(value, lambda h, y, c, l, x: (h, y, c, 1 - l, x))


def to_far_z(value):
    return permute(value, lambda h, y, c, l, x: (h + 1 if l else h - 1, y, c, 1 - l, x))


VMEM = pl.BlockSpec(memory_space=pltpu.VMEM)
SMEM = pl.BlockSpec(memory_space=pltpu.SMEM)
SMALL = pl.CostEstimate(flops=1000, bytes_accessed=1000, transcendentals=0)
PARAMS = pltpu.CompilerParams(vmem_limit_bytes=40 * 1024 * 1024)
BY_ROW = (((1,), (1,)), ((), ()))
BY_TOKEN = (((0,), (0,)), ((), ()))


def like(shape, dtype=BF16):
    return jax.ShapeDtypeStruct(shape, dtype)


def call(kernel, out_shape, *args, scalars=0):
    return pl.pallas_call(
        kernel,
        out_shape=out_shape,
        in_specs=[SMEM] * scalars + [VMEM] * (len(args) - scalars),
        out_specs=jax.tree.map(lambda _: VMEM, out_shape),
        compiler_params=PARAMS,
        cost_estimate=SMALL,
    )(*args)


def project_kernel(n_tiles, n_out, steps, *refs):
    tiles, (w_ref, f_ref), refs = refs[:n_tiles], refs[n_tiles : n_tiles + 2], refs[n_tiles + 2 :]
    outs, acc = refs[:n_out], refs[n_out]
    step = pl.program_id(0)
    tile = jnp.concatenate([t[...] for t in tiles], axis=0)
    for c in range(n_out):
        part = lax.dot_general(tile, w_ref[c] * f_ref[c], BY_ROW, preferred_element_type=F32)

        @pl.when(step == 0)
        def _():
            acc[c] = part

        @pl.when(step > 0)
        def _():
            acc[c] += part

        @pl.when(step == steps - 1)
        def _():
            outs[c][...] = acc[c].astype(BF16)


def project(tiles, w_t, factor, depth=1024):
    n, width, total = w_t.shape
    rows_ = sum(t.shape[0] for t in tiles)
    steps = total // depth
    return pl.pallas_call(
        functools.partial(project_kernel, len(tiles), n, steps),
        grid=(steps,),
        out_shape=[like((rows_, width))] * n,
        in_specs=[pl.BlockSpec((t.shape[0], depth), lambda k: (0, k)) for t in tiles]
        + [
            pl.BlockSpec((n, width, depth), lambda k: (0, 0, k)),
            pl.BlockSpec((n, 1, depth), lambda k: (0, 0, k)),
        ],
        out_specs=[pl.BlockSpec((rows_, width), lambda k: (0, 0))] * n,
        scratch_shapes=[pltpu.VMEM((n, rows_, width), F32)],
        compiler_params=PARAMS,
        cost_estimate=SMALL,
    )(*tiles, w_t, factor)


def grads_kernel(k1, k2, v1, v2, weight, gate_w, up_w, down_w, out):
    keys = jnp.concatenate([k1[...], k2[...]], axis=0)
    values = jnp.concatenate([v1[...], v2[...]], axis=0)
    gate = jnp.dot(keys, gate_w[...], preferred_element_type=F32)
    upper = jnp.dot(keys, up_w[...], preferred_element_type=F32)
    sigma = jax.nn.sigmoid(gate)
    active = gate * sigma
    hidden = (active * upper).astype(BF16)
    weighted = (weight[...] * values.astype(F32)).astype(BF16)
    d_hidden = jnp.dot(weighted, down_w[...], preferred_element_type=F32)
    d_gate = (d_hidden * upper * sigma * (1.0 + gate * (1.0 - sigma))).astype(BF16)
    d_upper = (d_hidden * active).astype(BF16)
    pairs = ((d_gate, keys), (d_upper, keys), (hidden, weighted))
    for i, (left, right) in enumerate(pairs):
        grad = lax.dot_general(left, right, BY_TOKEN, preferred_element_type=F32)
        out[:, i * 320 : (i + 1) * 320] = grad.astype(out.dtype)


def halves_kernel(y, own, got, to1, to2, to3, mine):
    for d, out in ((1, to1), (2, to2), (3, to3), (0, mine)):
        at = pl.ds(pl.multiple_of(lax.rem(y[0] + d, 4) * 80, 16), 80)
        out[...] = (own[at, :] + got[at, :].astype(F32)).astype(out.dtype)


def sum_kernel(mine, a, b, c, total, rounded):
    result = mine[...] + a[...].astype(F32) + b[...].astype(F32) + c[...].astype(F32)
    total[...] = result
    rounded[...] = result.astype(BF16)


def renorm_kernel(mine, a, b, c, old, out):
    total = mine[...] + a[...].astype(F32) + b[...].astype(F32) + c[...].astype(F32)
    before = old[...]
    fresh = before + total
    for i in range(3):
        at = slice(i * 320, (i + 1) * 320)
        old_norm = jnp.sqrt(jnp.sum(before[:, at] * before[:, at], axis=1, keepdims=True))
        new_sq = jnp.sum(fresh[:, at] * fresh[:, at], axis=1, keepdims=True)
        out[:, at] = (fresh[:, at] * (old_norm / jnp.sqrt(new_sq + 1e-06))).astype(BF16)


def respond_kernel(query_ref, column, other, *outs):
    renorm = jnp.concatenate([column[...], other[...]], axis=0)
    query = query_ref[...]
    gate = lax.dot_general(query, renorm[:, :320], BY_ROW, preferred_element_type=F32)
    upper = lax.dot_general(query, renorm[:, 320:640], BY_ROW, preferred_element_type=F32)
    hidden = (gate * jax.nn.sigmoid(gate) * upper).astype(BF16)
    output = jnp.dot(hidden, renorm[:, 640:], preferred_element_type=F32)
    scaled = output * lax.rsqrt(jnp.mean(output * output, axis=-1, keepdims=True) + 1e-05)
    answer = scaled.astype(BF16)
    at = 0
    for out in outs:
        out[...] = answer[at : at + out.shape[0]]
        at += out.shape[0]


def rows(value, start, size):
    return lax.dynamic_slice_in_dim(value, start, size, axis=0)


def gather(tokens):
    first, second = tokens[:32], tokens[32:]
    near_tile, far_tile = to_near_x(tokens), to_far_x(tokens)
    z1, z2 = to_near_z(first), to_far_z(second)
    opposite_first = to_far_x(near_tile[:32])
    opposite_second = to_near_x(far_tile[32:])
    z3 = to_near_z(jnp.concatenate([near_tile[:32], far_tile[:32]]))
    z4 = to_far_z(jnp.concatenate([near_tile[32:], far_tile[32:]]))
    z5, z6 = to_near_z(opposite_first), to_far_z(opposite_second)
    return (
        [tokens, near_tile, far_tile, opposite_first, opposite_second],
        [z1, z3, z5, z2, z4, z6],
    )


def x_order(x):
    return [x, x ^ 1, (x + jnp.where(x % 2 == 1, 1, 3)) % 4, (x + 2) % 4]


def weights_of_rows(weight, z_lo, x):
    tiles = weight.reshape(8, 64)
    same = lax.dynamic_slice_in_dim(tiles, z_lo * 4, 4, axis=0)
    other = lax.dynamic_slice_in_dim(tiles, (1 - z_lo) * 4, 4, axis=0)
    order = x_order(x)
    pick = lambda t: jnp.concatenate([lax.dynamic_slice_in_dim(t, i, 1, axis=0) for i in order])
    same, other = pick(same), pick(other)
    moved = permute(other[:, 32:], lambda h, y, c, l, x: (h - 1 if l else h + 1, y, c, l, x))
    return jnp.concatenate([same.reshape(256), other[:, :32].reshape(128), moved.reshape(128)])


def send_back(plane, for_near, for_far, z_lo, x):
    from_near = to_near_z(for_near).reshape(4, 32, 320)
    from_far = to_far_z(for_far).reshape(4, 32, 320)
    other = jnp.concatenate([from_near, from_far], axis=1)
    both = jnp.stack([plane.reshape(4, 64, 320), other], axis=1)
    slots = jnp.stack(
        [both[0], to_near_x(both[1]), to_far_x(both[2]), to_opposite_x(both[3])]
    ).reshape(8, 64, 320)
    out = []
    for head in range(8):
        d = (head % 4 - x) % 4
        at = jnp.where(d == 0, 0, jnp.where(d == 2, 3, jnp.where(head % 4 == x ^ 1, 1, 2)))
        slot = at * 2 + jnp.where(head // 4 == z_lo, 0, 1)
        out.append(lax.dynamic_slice_in_dim(slots, slot, 1, axis=0)[0])
    return jnp.concatenate(out, axis=1)


def body(tokens, w_qkv, scale_exp, gate_mask, rate, fast_gate, fast_up, fast_down):
    seq, head = lax.axis_index("seq"), lax.axis_index("head")
    core, y = seq % 2, (seq // 2) % 4
    z_lo, x = head // 4, head % 4
    factor = jnp.exp2(scale_exp.astype(F32)).astype(BF16)[:, :, 0]
    factor = jnp.repeat(factor, w_qkv.shape[1] // factor.shape[1], axis=1)[:, None, :]
    w_t = jnp.transpose(w_qkv, (0, 2, 1))
    weight = weights_of_rows(rate[0] * gate_mask[:, 0].astype(F32), z_lo, x)[:, None]
    old = (fast_gate[0], fast_up[0], fast_down[0])
    own_w = [lax.dynamic_slice_in_dim(w, core * 320, 320, axis=1) for w in old]
    other_w = [lax.dynamic_slice_in_dim(w, (1 - core) * 320, 320, axis=1) for w in old]
    old_t = rows(jnp.concatenate([w.T for w in own_w], axis=1), y * 80, 80).astype(F32)
    plane, others = gather(tokens)

    prepared = (weight, own_w, other_w, old_t, factor)
    plane, others[1], others[4], prepared = lax.optimization_barrier(
        (plane, others[1], others[4], prepared)
    )
    weight, own_w, other_w, old_t, factor = prepared
    ready = project(plane, w_t, factor)
    ready, others = lax.optimization_barrier((ready, others))
    keys, values = project(others, w_t[1:], factor[1:])

    inputs = (ready[1], keys, ready[2], values, weight)
    sent = call(grads_kernel, like((320, 960)), *inputs, *other_w)
    inputs, sent = lax.optimization_barrier((inputs, sent))
    got = to_core(sent)
    own = call(grads_kernel, like((320, 960), F32), *inputs, *own_w)
    own, got = lax.optimization_barrier((own, got))
    to1, to2, to3, mine = call(
        halves_kernel,
        [like((80, 960))] * 3 + [like((80, 960), F32)],
        y.astype(jnp.int32).reshape(1),
        own,
        got,
        scalars=1,
    )
    got = to_y(to2, 2), to_y(to1, 1), to_y(to3, 3)
    mine, small = call(sum_kernel, [like((80, 960), F32), like((80, 960))], mine, *got)

    others, small = lax.optimization_barrier((others, small))
    got = to_z(small, 2), to_z(small, 1), to_z(small, 3)
    (query_others,) = project(others, w_t[:1], factor[:1])
    query_others, got = lax.optimization_barrier((query_others, got))
    block = call(renorm_kernel, like((80, 960)), mine, *got, old_t)
    column = jnp.concatenate([block, to_y(block, 2), to_y(block, 1), to_y(block, 3)], axis=0)
    other = to_core(column)

    for_near, for_far = call(respond_kernel, [like((128, 320))] * 2, query_others, column, other)
    query_plane, for_near, for_far = lax.optimization_barrier((ready[0], for_near, for_far))
    (plane,) = call(respond_kernel, [like((256, 320))], query_plane, column, other)
    return send_back(plane, for_near, for_far, z_lo, x)


def solution(mesh):
    in_specs = (
        P(("seq", "head"), None),
        P(None, None, "head"),
        P(None, None, "head"),
        P("seq", "head"),
        P("head"),
        P("head", None, None),
        P("head", None, None),
        P("head", None, None),
    )
    out_specs = P(("seq", "head"), None)
    return jax.shard_map(body, mesh=mesh, in_specs=in_specs, out_specs=out_specs, check_vma=False)
```

```python
import functools

import jax
import jax.numpy as jnp
import numpy as np
from jax import lax
from jax.experimental import pallas as pl
from jax.experimental.pallas import tpu as pltpu
from jax.sharding import PartitionSpec as P

AXES = ("seq", "head")
BF16 = jnp.bfloat16
F32 = jnp.float32


def place(i):
    seq, head = divmod(i, 8)
    return seq // 8, (seq // 2) % 4, seq % 2, head // 4, head % 4


def permute(value, move):
    pairs = []
    for i in range(256):
        z_hi, y, core, z_lo, x = move(*place(i))
        pairs.append((i, ((z_hi % 4) * 8 + (y % 4) * 2 + core) * 8 + z_lo * 4 + x % 4))
    return lax.ppermute(value, AXES, pairs)


def to_core(value):
    return permute(value, lambda h, y, c, l, x: (h, y, 1 - c, l, x))


def to_y(value, d):
    return permute(value, lambda h, y, c, l, x: (h, y + d, c, l, x))


def to_z(value, d):
    return permute(value, lambda h, y, c, l, x: (h + d, y, c, l, x))


def near(x):
    return x ^ 1


def far(x):
    return (x + 1) % 4 if x % 2 else (x - 1) % 4


def to_near_x(value):
    return permute(value, lambda h, y, c, l, x: (h, y, c, l, near(x)))


def to_far_x(value):
    return permute(value, lambda h, y, c, l, x: (h, y, c, l, far(x)))


def to_opposite_x(value):
    return permute(value, lambda h, y, c, l, x: (h, y, c, l, x + 2))


def to_near_z(value):
    return permute(value, lambda h, y, c, l, x: (h, y, c, 1 - l, x))


def to_far_z(value):
    return permute(value, lambda h, y, c, l, x: (h + 1 if l else h - 1, y, c, 1 - l, x))


VMEM = pl.BlockSpec(memory_space=pltpu.VMEM)
SMEM = pl.BlockSpec(memory_space=pltpu.SMEM)
SMALL = pl.CostEstimate(flops=1000, bytes_accessed=1000, transcendentals=0)
PARAMS = pltpu.CompilerParams(vmem_limit_bytes=14 * 1024 * 1024)
BY_ROW = (((1,), (1,)), ((), ()))
BY_TOKEN = (((0,), (0,)), ((), ()))


def like(shape, dtype=BF16):
    return jax.ShapeDtypeStruct(shape, dtype)


def call(kernel, out_shape, *args, scalars=0, after=(), scratch=()):
    n, skip = len(args), len(args) + len(after)

    def run(*refs):
        kernel(*refs[:n], *refs[skip:])

    return pl.pallas_call(
        run,
        out_shape=out_shape,
        in_specs=[SMEM] * scalars + [VMEM] * (n - scalars) + [VMEM] * len(after),
        out_specs=jax.tree.map(lambda _: VMEM, out_shape),
        scratch_shapes=list(scratch),
        compiler_params=PARAMS,
        cost_estimate=SMALL,
    )(*args, *after)


def split_kernel(near_tile, far_tile, near_first, far_second, first, second):
    near_first[...] = near_tile[:32, :]
    far_second[...] = far_tile[32:, :]
    first[:32, :] = near_tile[:32, :]
    first[32:, :] = far_tile[:32, :]
    second[:32, :] = near_tile[32:, :]
    second[32:, :] = far_tile[32:, :]


def project_kernel(n_tiles, *refs):
    tile = jnp.concatenate([t[...] for t in refs[:n_tiles]], axis=0)
    w_ref, out = refs[n_tiles:]
    for c in range(w_ref.shape[0]):
        part = lax.dot_general(w_ref[c], tile, BY_ROW, preferred_element_type=F32)
        out[c * 320 : (c + 1) * 320, :] = part.astype(BF16)


def project(tiles, weff, after=()):
    shape = (weff.shape[0] * weff.shape[1], sum(t.shape[0] for t in tiles))
    return call(
        functools.partial(project_kernel, len(tiles)), like(shape), *tiles, weff, after=after
    )


def grads_kernel(which, my, kv1, kv2, weight, moved, gate_t, up_t, down_t, out):
    half = pl.ds(pl.multiple_of(my[which], 16), 320)
    weight = jnp.concatenate([weight[...], moved[...]], axis=1)
    keys = jnp.concatenate([kv1[:320, :], kv2[:320, :]], axis=1)
    values = jnp.concatenate([kv1[320:, :], kv2[320:, :]], axis=1)
    gate = jnp.dot(gate_t[half, :], keys, preferred_element_type=F32)
    upper = jnp.dot(up_t[half, :], keys, preferred_element_type=F32)
    sigma = jax.nn.sigmoid(gate)
    active = gate * sigma
    hidden = (active * upper).astype(BF16)
    weighted = (weight * values.astype(F32)).astype(BF16)
    d_hidden = jnp.dot(down_t[half, :], weighted, preferred_element_type=F32)
    d_gate = (d_hidden * upper * sigma * (1.0 + gate * (1.0 - sigma))).astype(BF16)
    d_upper = (d_hidden * active).astype(BF16)
    pairs = ((d_gate, keys), (d_upper, keys), (hidden, weighted))
    for i, (left, right) in enumerate(pairs):
        grad = lax.dot_general(left, right, BY_ROW, preferred_element_type=F32)
        out[:, i * 320 : (i + 1) * 320] = grad.astype(out.dtype)


def halves_kernel(my, own, got, to1, to2, to3, mine):
    for d, out in ((1, to1), (2, to2), (3, to3), (0, mine)):
        at = pl.ds(pl.multiple_of(lax.rem(my[Y] + d, 4) * 80, 16), 80)
        out[...] = (own[at, :] + got[at, :].astype(F32)).astype(out.dtype)


def sum_kernel(mine, a, b, c, total, rounded):
    result = mine[...] + a[...].astype(F32) + b[...].astype(F32) + c[...].astype(F32)
    total[...] = result
    rounded[...] = result.astype(BF16)


def renorm_kernel(my, mine, a, b, c, gate_t, up_t, down_t, out):
    total = mine[...] + a[...].astype(F32) + b[...].astype(F32) + c[...].astype(F32)
    mine_rows = pl.ds(pl.multiple_of(my[BLOCK], 16), 80)
    for i, old in enumerate((gate_t, up_t, down_t)):
        at = slice(i * 320, (i + 1) * 320)
        before = old[mine_rows, :].astype(F32)
        fresh = before + total[:, at]
        old_norm = jnp.sqrt(jnp.sum(before * before, axis=1, keepdims=True))
        new_sq = jnp.sum(fresh * fresh, axis=1, keepdims=True)
        out[:, at] = (fresh * (old_norm / jnp.sqrt(new_sq + 1e-06))).astype(BF16)


def respond_kernel(start, query_ref, column, other, *outs):
    renorm = jnp.concatenate([column[...], other[...]], axis=0)
    query = query_ref[:, start : start + 256]
    gate = jnp.dot(renorm[:, :320], query, preferred_element_type=F32)
    upper = jnp.dot(renorm[:, 320:640], query, preferred_element_type=F32)
    hidden = (gate * jax.nn.sigmoid(gate) * upper).astype(BF16)
    output = lax.dot_general(hidden, renorm[:, 640:], BY_TOKEN, preferred_element_type=F32)
    scaled = output * lax.rsqrt(jnp.mean(output * output, axis=-1, keepdims=True) + 1e-05)
    answer = scaled.astype(BF16)
    at = 0
    for out in outs:
        out[...] = answer[at : at + out.shape[0]]
        at += out.shape[0]


def gather(tokens, work):
    near_tile, far_tile = to_near_x(tokens), to_far_x(tokens)
    z1, z2 = to_near_z(tokens[:32]), to_far_z(tokens[32:])
    near_first, far_second, first, second = call(
        split_kernel,
        [like((32, 5120)), like((32, 5120)), like((64, 5120)), like((64, 5120))],
        near_tile,
        far_tile,
        after=(z1, z2, *work),
    )
    opposite_first, opposite_second = to_far_x(near_first), to_near_x(far_second)
    z3, z4 = to_near_z(first), to_far_z(second)
    z5, z6 = to_near_z(opposite_first), to_far_z(opposite_second)
    return (
        [tokens, near_tile, far_tile, opposite_first, opposite_second],
        [z1, z3, z5, z2, z4, z6],
    )


OWN_HALF, OTHER_HALF, Y, BLOCK, SAME, OTHER, SLOT = 0, 1, 2, 3, 4, 8, 12


def table():
    lines = np.zeros((256, 32), np.int32)
    for i in range(256):
        _, y, core, z_lo, x = place(i)
        order = [x, near(x), far(x), (x + 2) % 4]
        lines[i, :4] = core * 320, 320 - core * 320, y, core * 320 + y * 80
        lines[i, SAME : SAME + 4] = [z_lo * 4 + t for t in order]
        lines[i, OTHER : OTHER + 4] = [(1 - z_lo) * 4 + t for t in order]
        lines[i, SLOT : SLOT + 8] = [order.index(h % 4) * 2 + (h // 4 != z_lo) for h in range(8)]
    return lines


def weights_kernel(my, rate, mask, weight, sent):
    for i in range(4):
        same = mask[pl.ds(my[SAME + i], 1), :].astype(F32) * rate[0]
        other = mask[pl.ds(my[OTHER + i], 1), :].astype(F32) * rate[0]
        weight[:, i * 64 : (i + 1) * 64] = same
        weight[:, 256 + i * 32 : 288 + i * 32] = other[:, :32]
        sent[:, i * 32 : (i + 1) * 32] = other[:, 32:]


def pieces_kernel(plane, from_near, from_far, *outs):
    for i, out in enumerate(outs):
        out[0] = plane[i * 64 : (i + 1) * 64, :]
        out[1, :32] = from_near[i * 32 : (i + 1) * 32, :]
        out[1, 32:] = from_far[i * 32 : (i + 1) * 32, :]


def place_kernel(my, a, b, c, d, out, slots):
    for i, piece in enumerate((a, b, c, d)):
        slots[2 * i : 2 * i + 2] = piece[...]
    for head in range(8):
        out[:, head * 320 : (head + 1) * 320] = slots[my[SLOT + head]]


def send_back(my, plane, for_near, for_far):
    pieces = call(
        pieces_kernel, [like((2, 64, 320))] * 4, plane, to_near_z(for_near), to_far_z(for_far)
    )
    opposite = to_opposite_x(pieces[3])
    pieces = pieces[0], to_near_x(pieces[1]), to_far_x(pieces[2]), opposite
    return call(
        place_kernel,
        like((64, 2560)),
        my,
        *pieces,
        scalars=1,
        scratch=[pltpu.VMEM((8, 64, 320), BF16)],
    )


def body(tokens, w_qkv, scale_exp, gate_mask, rate, fast_gate, fast_up, fast_down):
    at = lax.axis_index("seq") * 8 + lax.axis_index("head")
    my = lax.dynamic_slice_in_dim(jnp.asarray(table()), at, 1, axis=0).reshape(32)
    tokens, my = lax.optimization_barrier((tokens, my))
    factor = jnp.exp2(scale_exp.astype(F32)).astype(BF16)[:, :, 0]
    factor = jnp.repeat(factor, w_qkv.shape[1] // factor.shape[1], axis=1)[:, None, :]
    w_t = jnp.transpose(w_qkv, (0, 2, 1))
    weight, sent = call(
        weights_kernel,
        [like((1, 384), F32), like((1, 128), F32)],
        my,
        rate,
        gate_mask.reshape(8, 64),
        scalars=2,
    )
    moved = permute(sent, lambda h, y, c, l, x: (h - 1 if l else h + 1, y, c, l, x))
    old_t = [w[0].T for w in (fast_gate, fast_up, fast_down)]
    weff_kv, weff_q = w_t[1:] * factor[1:], w_t[:1] * factor[:1]
    plane, others = gather(tokens, (weff_kv[0, :8, :128], weight, *old_t))
    kv1 = project(plane, weff_kv, after=(others[1], others[4]))
    kv2 = project(others, weff_kv, after=(kv1,))

    grads = (my, kv1, kv2, weight, moved, *old_t)
    sent = call(
        functools.partial(grads_kernel, OTHER_HALF), like((320, 960)), *grads, scalars=1
    )
    got = to_core(sent)
    own = call(
        functools.partial(grads_kernel, OWN_HALF),
        like((320, 960), F32),
        *grads,
        scalars=1,
        after=(sent,),
    )
    to1, to2, to3, mine = call(
        halves_kernel, [like((80, 960))] * 3 + [like((80, 960), F32)], my, own, got, scalars=1
    )
    got = to_y(to2, 2), to_y(to1, 1), to_y(to3, 3)
    mine, small = call(sum_kernel, [like((80, 960), F32), like((80, 960))], mine, *got)

    got = to_z(small, 2), to_z(small, 1), to_z(small, 3)
    query = project(plane + others, weff_q, after=(small,))
    block = call(
        renorm_kernel,
        like((80, 960)),
        my,
        mine,
        *got,
        *old_t,
        scalars=1,
        after=(query,),
    )
    column = jnp.concatenate([block, to_y(block, 2), to_y(block, 1), to_y(block, 3)], axis=0)
    other = to_core(column)

    for_near, for_far = call(
        functools.partial(respond_kernel, 256), [like((128, 320))] * 2, query, column, other
    )
    (answers,) = call(
        functools.partial(respond_kernel, 0),
        [like((256, 320))],
        query,
        column,
        other,
        after=(for_near,),
    )
    return send_back(my, answers, for_near, for_far)


def solution(mesh):
    in_specs = (
        P(("seq", "head"), None),
        P(None, None, "head"),
        P(None, None, "head"),
        P("seq", "head"),
        P("head"),
        P("head", None, None),
        P("head", None, None),
        P("head", None, None),
    )
    out_specs = P(("seq", "head"), None)
    return jax.shard_map(body, mesh=mesh, in_specs=in_specs, out_specs=out_specs, check_vma=False)
```

```python
import functools

import jax
import jax.numpy as jnp
import numpy as np
from jax import lax
from jax.experimental import pallas as pl
from jax.experimental.pallas import tpu as pltpu
from jax.sharding import PartitionSpec as P

AXES = ("seq", "head")
BF16 = jnp.bfloat16
F32 = jnp.float32


def place(i):
    seq, head = divmod(i, 8)
    return seq // 8, (seq // 2) % 4, seq % 2, head // 4, head % 4


def permute(value, move):
    pairs = []
    for i in range(256):
        z_hi, y, core, z_lo, x = move(*place(i))
        pairs.append((i, ((z_hi % 4) * 8 + (y % 4) * 2 + core) * 8 + z_lo * 4 + x % 4))
    return lax.ppermute(value, AXES, pairs)


def to_core(value):
    return permute(value, lambda h, y, c, l, x: (h, y, 1 - c, l, x))


def to_y(value, d):
    return permute(value, lambda h, y, c, l, x: (h, y + d, c, l, x))


def to_z(value, d):
    return permute(value, lambda h, y, c, l, x: (h + d, y, c, l, x))


def near(x):
    return x ^ 1


def far(x):
    return (x + 1) % 4 if x % 2 else (x - 1) % 4


def to_near_x(value):
    return permute(value, lambda h, y, c, l, x: (h, y, c, l, near(x)))


def to_far_x(value):
    return permute(value, lambda h, y, c, l, x: (h, y, c, l, far(x)))


def to_opposite_x(value):
    return permute(value, lambda h, y, c, l, x: (h, y, c, l, x + 2))


def to_near_z(value):
    return permute(value, lambda h, y, c, l, x: (h, y, c, 1 - l, x))


def to_far_z(value):
    return permute(value, lambda h, y, c, l, x: (h + 1 if l else h - 1, y, c, 1 - l, x))


VMEM = pl.BlockSpec(memory_space=pltpu.VMEM)
SMEM = pl.BlockSpec(memory_space=pltpu.SMEM)
SMALL = pl.CostEstimate(flops=1000, bytes_accessed=1000, transcendentals=0)
PARAMS = pltpu.CompilerParams(vmem_limit_bytes=20 * 1024 * 1024)
BY_ROW = (((1,), (1,)), ((), ()))
BY_TOKEN = (((0,), (0,)), ((), ()))


def like(shape, dtype=BF16):
    return jax.ShapeDtypeStruct(shape, dtype)


def call(kernel, out_shape, *args, scalars=0, after=(), scratch=()):
    n, skip = len(args), len(args) + len(after)

    def run(*refs):
        kernel(*refs[:n], *refs[skip:])

    return pl.pallas_call(
        run,
        out_shape=out_shape,
        in_specs=[SMEM] * scalars + [VMEM] * (n - scalars) + [VMEM] * len(after),
        out_specs=jax.tree.map(lambda _: VMEM, out_shape),
        scratch_shapes=list(scratch),
        compiler_params=PARAMS,
        cost_estimate=SMALL,
    )(*args, *after)


def split_kernel(near_tile, far_tile, z1, z2, near_first, far_second, first, second, both):
    near_first[...] = near_tile[:32, :]
    far_second[...] = far_tile[32:, :]
    first[:16, :] = near_tile[16:32, :]
    first[16:, :] = far_tile[16:32, :]
    second[:16, :] = near_tile[48:, :]
    second[16:, :] = far_tile[48:, :]
    both[:16, :] = z1[:16, :]
    both[16:, :] = z2[:16, :]


def project_kernel(cuts, first, count, *refs):
    tiles, (w_ref, f_ref, out) = refs[:-3], refs[-3:]
    tile = jnp.concatenate([tiles[i][lo:hi, :] for i, lo, hi in cuts], axis=0)
    for c in range(count):
        weff = w_ref[first + c] * f_ref[first + c]
        part = lax.dot_general(weff, tile, BY_ROW, preferred_element_type=F32)
        out[c * 320 : (c + 1) * 320, :] = part.astype(BF16)


def project(tiles, cuts, w_t, factor, first, count, after=()):
    shape = (count * w_t.shape[1], sum(hi - lo for _, lo, hi in cuts))
    kernel = functools.partial(project_kernel, cuts, first, count)
    return call(kernel, like(shape), *tiles, w_t, factor, after=after)


def grads_kernel(which, my, kv1, kv2, weight, moved, gate_t, up_t, down_t, out):
    half = pl.ds(pl.multiple_of(my[which], 16), 320)
    weight = jnp.concatenate([weight[...], moved[...]], axis=1)
    keys = jnp.concatenate([kv1[:320, :], kv2[:320, :]], axis=1)
    values = jnp.concatenate([kv1[320:, :], kv2[320:, :]], axis=1)
    gate = jnp.dot(gate_t[half, :], keys, preferred_element_type=F32)
    upper = jnp.dot(up_t[half, :], keys, preferred_element_type=F32)
    sigma = jax.nn.sigmoid(gate)
    active = gate * sigma
    hidden = (active * upper).astype(BF16)
    weighted = (weight * values.astype(F32)).astype(BF16)
    d_hidden = jnp.dot(down_t[half, :], weighted, preferred_element_type=F32)
    d_gate = (d_hidden * upper * sigma * (1.0 + gate * (1.0 - sigma))).astype(BF16)
    d_upper = (d_hidden * active).astype(BF16)
    pairs = ((d_gate, keys), (d_upper, keys), (hidden, weighted))
    for i, (left, right) in enumerate(pairs):
        grad = lax.dot_general(left, right, BY_ROW, preferred_element_type=F32)
        out[:, i * 320 : (i + 1) * 320] = grad.astype(out.dtype)


def halves_kernel(my, own, got, to1, to2, to3, mine):
    for d, out in ((1, to1), (2, to2), (3, to3), (0, mine)):
        at = pl.ds(pl.multiple_of(lax.rem(my[Y] + d, 4) * 80, 16), 80)
        out[...] = (own[at, :] + got[at, :].astype(F32)).astype(out.dtype)


def sum_kernel(mine, a, b, c, total, rounded):
    result = mine[...] + a[...].astype(F32) + b[...].astype(F32) + c[...].astype(F32)
    total[...] = result
    rounded[...] = result.astype(BF16)


def renorm_kernel(my, mine, a, b, c, gate_t, up_t, down_t, out):
    total = mine[...] + a[...].astype(F32) + b[...].astype(F32) + c[...].astype(F32)
    mine_rows = pl.ds(pl.multiple_of(my[BLOCK], 16), 80)
    for i, old in enumerate((gate_t, up_t, down_t)):
        at = slice(i * 320, (i + 1) * 320)
        before = old[mine_rows, :].astype(F32)
        fresh = before + total[:, at]
        old_norm = jnp.sqrt(jnp.sum(before * before, axis=1, keepdims=True))
        new_sq = jnp.sum(fresh * fresh, axis=1, keepdims=True)
        out[:, at] = (fresh * (old_norm / jnp.sqrt(new_sq + 1e-06))).astype(BF16)


def respond_kernel(start, query_ref, column, other, *outs):
    renorm = jnp.concatenate([column[...], other[...]], axis=0)
    query = query_ref[:, start : start + 256]
    gate = jnp.dot(renorm[:, :320], query, preferred_element_type=F32)
    upper = jnp.dot(renorm[:, 320:640], query, preferred_element_type=F32)
    hidden = (gate * jax.nn.sigmoid(gate) * upper).astype(BF16)
    output = lax.dot_general(hidden, renorm[:, 640:], BY_TOKEN, preferred_element_type=F32)
    scaled = output * lax.rsqrt(jnp.mean(output * output, axis=-1, keepdims=True) + 1e-05)
    answer = scaled.astype(BF16)
    at = 0
    for out in outs:
        out[...] = answer[at : at + out.shape[0]]
        at += out.shape[0]


PLANE = [(0, 0, 64), (1, 0, 64), (2, 0, 64), (3, 0, 32), (4, 0, 32)]
OTHERS = [(0, 0, 32), (2, 0, 16), (4, 0, 16), (3, 0, 16), (4, 16, 32), (6, 0, 32)]
OTHERS += [(1, 0, 32), (2, 16, 32), (5, 0, 16), (3, 16, 32), (5, 16, 32), (7, 0, 32)]


def gather(tokens, work):
    near_tile, far_tile = to_near_x(tokens), to_far_x(tokens)
    z1, z2 = to_near_z(tokens[:32]), to_far_z(tokens[32:])
    near_first, far_second, first, second, both = call(
        split_kernel, [like((32, 5120))] * 5, near_tile, far_tile, z1, z2, after=work
    )
    opposite_first, opposite_second = to_far_x(near_first), to_near_x(far_second)
    z3, z4 = to_near_z(first), to_far_z(second)
    near_both, far_both = to_near_x(both), to_far_x(both)
    z5, z6 = to_near_z(opposite_first), to_far_z(opposite_second)
    return (
        [tokens, near_tile, far_tile, opposite_first, opposite_second],
        [z1, z2, near_both, far_both, z3, z4, z5, z6],
    )


OWN_HALF, OTHER_HALF, Y, BLOCK, SAME, OTHER, SLOT = 0, 1, 2, 3, 4, 8, 12


def table():
    lines = np.zeros((256, 32), np.int32)
    for i in range(256):
        _, y, core, z_lo, x = place(i)
        order = [x, near(x), far(x), (x + 2) % 4]
        lines[i, :4] = core * 320, 320 - core * 320, y, core * 320 + y * 80
        lines[i, SAME : SAME + 4] = [z_lo * 4 + t for t in order]
        lines[i, OTHER : OTHER + 4] = [(1 - z_lo) * 4 + t for t in order]
        lines[i, SLOT : SLOT + 8] = [order.index(h % 4) * 2 + (h // 4 != z_lo) for h in range(8)]
    return lines


def weights_kernel(my, rate, mask, weight, sent):
    for i in range(4):
        same = mask[pl.ds(my[SAME + i], 1), :].astype(F32) * rate[0]
        other = mask[pl.ds(my[OTHER + i], 1), :].astype(F32) * rate[0]
        weight[:, i * 64 : (i + 1) * 64] = same
        weight[:, 256 + i * 32 : 288 + i * 32] = other[:, :32]
        sent[:, i * 32 : (i + 1) * 32] = other[:, 32:]


def pieces_kernel(plane, from_near, from_far, *outs):
    for i, out in enumerate(outs):
        out[0] = plane[i * 64 : (i + 1) * 64, :]
        out[1, :32] = from_near[i * 32 : (i + 1) * 32, :]
        out[1, 32:] = from_far[i * 32 : (i + 1) * 32, :]


def place_kernel(my, a, b, c, d, out, slots):
    for i, piece in enumerate((a, b, c, d)):
        slots[2 * i : 2 * i + 2] = piece[...]
    for head in range(8):
        out[:, head * 320 : (head + 1) * 320] = slots[my[SLOT + head]]


def send_back(my, plane, for_near, for_far):
    pieces = call(
        pieces_kernel, [like((2, 64, 320))] * 4, plane, to_near_z(for_near), to_far_z(for_far)
    )
    opposite = to_opposite_x(pieces[3])
    pieces = pieces[0], to_near_x(pieces[1]), to_far_x(pieces[2]), opposite
    return call(
        place_kernel,
        like((64, 2560)),
        my,
        *pieces,
        scalars=1,
        scratch=[pltpu.VMEM((8, 64, 320), BF16)],
    )


def body(tokens, w_qkv, scale_exp, gate_mask, rate, fast_gate, fast_up, fast_down):
    at = lax.axis_index("seq") * 8 + lax.axis_index("head")
    my = lax.dynamic_slice_in_dim(jnp.asarray(table()), at, 1, axis=0).reshape(32)
    tokens, my = lax.optimization_barrier((tokens, my))
    factor = jnp.exp2(scale_exp.astype(F32)).astype(BF16)[:, :, 0]
    factor = jnp.repeat(factor, w_qkv.shape[1] // factor.shape[1], axis=1)[:, None, :]
    w_t = jnp.transpose(w_qkv, (0, 2, 1))
    weight, sent = call(
        weights_kernel,
        [like((1, 384), F32), like((1, 128), F32)],
        my,
        rate,
        gate_mask.reshape(8, 64),
        scalars=2,
    )
    moved = permute(sent, lambda h, y, c, l, x: (h - 1 if l else h + 1, y, c, l, x))
    old_t = [w[0].T for w in (fast_gate, fast_up, fast_down)]
    plane, others = gather(tokens, (factor, weight, *old_t))
    kv1 = project(plane, PLANE, w_t, factor, 1, 2, after=others[2:6])
    kv2 = project(others, OTHERS, w_t, factor, 1, 2, after=(kv1,))

    grads = (my, kv1, kv2, weight, moved, *old_t)
    sent = call(
        functools.partial(grads_kernel, OTHER_HALF), like((320, 960)), *grads, scalars=1
    )
    got = to_core(sent)
    own = call(
        functools.partial(grads_kernel, OWN_HALF),
        like((320, 960), F32),
        *grads,
        scalars=1,
        after=(sent,),
    )
    to1, to2, to3, mine = call(
        halves_kernel, [like((80, 960))] * 3 + [like((80, 960), F32)], my, own, got, scalars=1
    )
    got = to_y(to2, 2), to_y(to1, 1), to_y(to3, 3)
    mine, small = call(sum_kernel, [like((80, 960), F32), like((80, 960))], mine, *got)

    got = to_z(small, 2), to_z(small, 1), to_z(small, 3)
    cuts = PLANE + [(len(plane) + i, lo, hi) for i, lo, hi in OTHERS]
    query = project(plane + others, cuts, w_t, factor, 0, 1, after=(small,))
    block = call(
        renorm_kernel,
        like((80, 960)),
        my,
        mine,
        *got,
        *old_t,
        scalars=1,
        after=(query,),
    )
    column = jnp.concatenate([block, to_y(block, 2), to_y(block, 1), to_y(block, 3)], axis=0)
    other = to_core(column)

    for_near, for_far = call(
        functools.partial(respond_kernel, 256), [like((128, 320))] * 2, query, column, other
    )
    (answers,) = call(
        functools.partial(respond_kernel, 0),
        [like((256, 320))],
        query,
        column,
        other,
        after=(for_near,),
    )
    return send_back(my, answers, for_near, for_far)


def solution(mesh):
    in_specs = (
        P(("seq", "head"), None),
        P(None, None, "head"),
        P(None, None, "head"),
        P("seq", "head"),
        P("head"),
        P("head", None, None),
        P("head", None, None),
        P("head", None, None),
    )
    out_specs = P(("seq", "head"), None)
    return jax.shard_map(body, mesh=mesh, in_specs=in_specs, out_specs=out_specs, check_vma=False)
```

```python
import functools

import jax
import jax.numpy as jnp
import numpy as np
from jax import lax
from jax.experimental import pallas as pl
from jax.experimental.pallas import tpu as pltpu
from jax.sharding import PartitionSpec as P

AXES = ("seq", "head")
BF16 = jnp.bfloat16
F32 = jnp.float32


def place(i):
    seq, head = divmod(i, 8)
    return seq // 8, (seq // 2) % 4, seq % 2, head // 4, head % 4


def permute(value, move):
    pairs = []
    for i in range(256):
        z_hi, y, core, z_lo, x = move(*place(i))
        pairs.append((i, ((z_hi % 4) * 8 + (y % 4) * 2 + core) * 8 + z_lo * 4 + x % 4))
    return lax.ppermute(value, AXES, pairs)


def to_core(value):
    return permute(value, lambda h, y, c, l, x: (h, y, 1 - c, l, x))


def to_y(value, d):
    return permute(value, lambda h, y, c, l, x: (h, y + d, c, l, x))


def to_near_h(value):
    return permute(value, lambda h, y, c, l, x: (near(h), y, c, l, x))


def to_far_h(value):
    return permute(value, lambda h, y, c, l, x: (far(h), y, c, l, x))


def near(x):
    return x ^ 1


def far(x):
    return (x + 1) % 4 if x % 2 else (x - 1) % 4


def to_near_x(value):
    return permute(value, lambda h, y, c, l, x: (h, y, c, l, near(x)))


def to_far_x(value):
    return permute(value, lambda h, y, c, l, x: (h, y, c, l, far(x)))


def to_opposite_x(value):
    return permute(value, lambda h, y, c, l, x: (h, y, c, l, x + 2))


def to_near_z(value):
    return permute(value, lambda h, y, c, l, x: (h, y, c, 1 - l, x))


def to_far_z(value):
    return permute(value, lambda h, y, c, l, x: (h + 1 if l else h - 1, y, c, 1 - l, x))


VMEM = pl.BlockSpec(memory_space=pltpu.VMEM)
SMEM = pl.BlockSpec(memory_space=pltpu.SMEM)
SMALL = pl.CostEstimate(flops=1000, bytes_accessed=1000, transcendentals=0)
PARAMS = pltpu.CompilerParams(vmem_limit_bytes=20 * 1024 * 1024)
BY_ROW = (((1,), (1,)), ((), ()))
BY_TOKEN = (((0,), (0,)), ((), ()))


def like(shape, dtype=BF16):
    return jax.ShapeDtypeStruct(shape, dtype)


def call(kernel, out_shape, *args, scalars=0, after=(), scratch=()):
    n, skip = len(args), len(args) + len(after)

    def run(*refs):
        kernel(*refs[:n], *refs[skip:])

    return pl.pallas_call(
        run,
        out_shape=out_shape,
        in_specs=[SMEM] * scalars + [VMEM] * (n - scalars) + [VMEM] * len(after),
        out_specs=jax.tree.map(lambda _: VMEM, out_shape),
        scratch_shapes=list(scratch),
        compiler_params=PARAMS,
        cost_estimate=SMALL,
    )(*args, *after)


def split_kernel(near_tile, far_tile, z1, z2, near_first, far_second, first, second, both):
    near_first[...] = near_tile[:32, :]
    far_second[...] = far_tile[32:, :]
    first[:16, :] = near_tile[16:32, :]
    first[16:, :] = far_tile[16:32, :]
    second[:16, :] = near_tile[48:, :]
    second[16:, :] = far_tile[48:, :]
    both[:16, :] = z1[:16, :]
    both[16:, :] = z2[:16, :]


def load_kernel(first, w_hbm, f_ref, out, sems):
    copies = []
    for c in range(out.shape[0]):
        for i in range(4):
            at = pl.ds(i * 80, 80)
            source, target = w_hbm.at[first + c, at, :], out.at[c, at, :]
            copies.append((c, at, pltpu.make_async_copy(source, target, sems.at[c * 4 + i])))
    for _, _, copy in copies:
        copy.start()
    for c, at, copy in copies:
        copy.wait()
        out[c, at, :] = out[c, at, :] * f_ref[first + c]


def load(w_t, factor, first, count, after=()):
    def run(*refs):
        load_kernel(first, *refs[:2], *refs[-2:])

    return pl.pallas_call(
        run,
        out_shape=like((count, *w_t.shape[1:])),
        in_specs=[pl.BlockSpec(memory_space=pl.ANY), VMEM] + [VMEM] * len(after),
        out_specs=VMEM,
        scratch_shapes=[pltpu.SemaphoreType.DMA((count * 4,))],
        compiler_params=pltpu.CompilerParams(vmem_limit_bytes=44 * 1024 * 1024),
        cost_estimate=SMALL,
    )(w_t, factor, *after)


def project_kernel(cuts, *refs):
    tiles, (w_ref, out) = refs[:-2], refs[-2:]
    tile = jnp.concatenate([tiles[i][lo:hi, :] for i, lo, hi in cuts], axis=0)
    for c in range(w_ref.shape[0]):
        part = lax.dot_general(w_ref[c], tile, BY_ROW, preferred_element_type=F32)
        out[c * 320 : (c + 1) * 320, :] = part.astype(BF16)


def project(tiles, cuts, weff, after=()):
    shape = (weff.shape[0] * weff.shape[1], sum(hi - lo for _, lo, hi in cuts))
    return call(functools.partial(project_kernel, cuts), like(shape), *tiles, weff, after=after)


def grads_kernel(which, my, kv1, kv2, weight, moved, gate_t, up_t, down_t, out):
    half = pl.ds(pl.multiple_of(my[which], 16), 320)
    weight = jnp.concatenate([weight[...], moved[...]], axis=1)
    keys = jnp.concatenate([kv1[:320, :], kv2[:320, :]], axis=1)
    values = jnp.concatenate([kv1[320:, :], kv2[320:, :]], axis=1)
    gate = jnp.dot(gate_t[half, :], keys, preferred_element_type=F32)
    upper = jnp.dot(up_t[half, :], keys, preferred_element_type=F32)
    sigma = jax.nn.sigmoid(gate)
    active = gate * sigma
    hidden = (active * upper).astype(BF16)
    weighted = (weight * values.astype(F32)).astype(BF16)
    d_hidden = jnp.dot(down_t[half, :], weighted, preferred_element_type=F32)
    d_gate = (d_hidden * upper * sigma * (1.0 + gate * (1.0 - sigma))).astype(BF16)
    d_upper = (d_hidden * active).astype(BF16)
    pairs = ((d_gate, keys), (d_upper, keys), (hidden, weighted))
    for i, (left, right) in enumerate(pairs):
        grad = lax.dot_general(left, right, BY_ROW, preferred_element_type=F32)
        out[:, i * 320 : (i + 1) * 320] = grad.astype(out.dtype)


def halves_kernel(my, own, got, to1, to2, to3, mine):
    for d, out in ((1, to1), (2, to2), (3, to3), (0, mine)):
        at = pl.ds(pl.multiple_of(lax.rem(my[Y] + d, 4) * 80, 16), 80)
        out[...] = (own[at, :] + got[at, :].astype(F32)).astype(out.dtype)


def sum_kernel(mine, a, b, c, total, upper, lower):
    result = mine[...] + a[...].astype(F32) + b[...].astype(F32) + c[...].astype(F32)
    total[...] = result
    upper[...] = result[:40].astype(BF16)
    lower[...] = result[40:].astype(BF16)


def pair_kernel(mine, a, b, total, upper, lower):
    total[:40, :] = mine[:40, :] + a[...].astype(F32)
    total[40:, :] = mine[40:, :] + b[...].astype(F32)
    upper[...] = total[:40, :].astype(BF16)
    lower[...] = total[40:, :].astype(BF16)


def renorm_kernel(my, mine, a, b, gate_t, up_t, down_t, out):
    got = jnp.concatenate([a[...].astype(F32), b[...].astype(F32)], axis=0)
    total = mine[...] + got
    mine_rows = pl.ds(pl.multiple_of(my[BLOCK], 16), 80)
    for i, old in enumerate((gate_t, up_t, down_t)):
        at = slice(i * 320, (i + 1) * 320)
        before = old[mine_rows, :].astype(F32)
        fresh = before + total[:, at]
        old_norm = jnp.sqrt(jnp.sum(before * before, axis=1, keepdims=True))
        new_sq = jnp.sum(fresh * fresh, axis=1, keepdims=True)
        out[:, at] = (fresh * (old_norm / jnp.sqrt(new_sq + 1e-06))).astype(BF16)


def respond_kernel(start, query_ref, column, other, *outs):
    renorm = jnp.concatenate([column[...], other[...]], axis=0)
    query = query_ref[:, start : start + 256]
    gate = jnp.dot(renorm[:, :320], query, preferred_element_type=F32)
    upper = jnp.dot(renorm[:, 320:640], query, preferred_element_type=F32)
    hidden = (gate * jax.nn.sigmoid(gate) * upper).astype(BF16)
    output = lax.dot_general(hidden, renorm[:, 640:], BY_TOKEN, preferred_element_type=F32)
    scaled = output * lax.rsqrt(jnp.mean(output * output, axis=-1, keepdims=True) + 1e-05)
    answer = scaled.astype(BF16)
    at = 0
    for out in outs:
        out[...] = answer[at : at + out.shape[0]]
        at += out.shape[0]


PLANE = [(0, 0, 64), (1, 0, 64), (2, 0, 64), (3, 0, 32), (4, 0, 32)]
OTHERS = [(0, 0, 32), (2, 0, 16), (4, 0, 16), (3, 0, 16), (4, 16, 32), (6, 0, 32)]
OTHERS += [(1, 0, 32), (2, 16, 32), (5, 0, 16), (3, 16, 32), (5, 16, 32), (7, 0, 32)]


def gather(tokens, work):
    near_tile, far_tile = to_near_x(tokens), to_far_x(tokens)
    z1, z2 = to_near_z(tokens[:32]), to_far_z(tokens[32:])
    near_first, far_second, first, second, both = call(
        split_kernel, [like((32, 5120))] * 5, near_tile, far_tile, z1, z2, after=work
    )
    opposite_first, opposite_second = to_far_x(near_first), to_near_x(far_second)
    z3, z4 = to_near_z(first), to_far_z(second)
    near_both, far_both = to_near_x(both), to_far_x(both)
    z5, z6 = to_near_z(opposite_first), to_far_z(opposite_second)
    return (
        [tokens, near_tile, far_tile, opposite_first, opposite_second],
        [z1, z2, near_both, far_both, z3, z4, z5, z6],
    )


OWN_HALF, OTHER_HALF, Y, BLOCK, SAME, OTHER, SLOT = 0, 1, 2, 3, 4, 8, 12


def table():
    lines = np.zeros((256, 32), np.int32)
    for i in range(256):
        _, y, core, z_lo, x = place(i)
        order = [x, near(x), far(x), (x + 2) % 4]
        lines[i, :4] = core * 320, 320 - core * 320, y, core * 320 + y * 80
        lines[i, SAME : SAME + 4] = [z_lo * 4 + t for t in order]
        lines[i, OTHER : OTHER + 4] = [(1 - z_lo) * 4 + t for t in order]
        lines[i, SLOT : SLOT + 8] = [order.index(h % 4) * 2 + (h // 4 != z_lo) for h in range(8)]
    return lines


def weights_kernel(my, rate, mask, weight, sent):
    for i in range(4):
        same = mask[pl.ds(my[SAME + i], 1), :].astype(F32) * rate[0]
        other = mask[pl.ds(my[OTHER + i], 1), :].astype(F32) * rate[0]
        weight[:, i * 64 : (i + 1) * 64] = same
        weight[:, 256 + i * 32 : 288 + i * 32] = other[:, :32]
        sent[:, i * 32 : (i + 1) * 32] = other[:, 32:]


def pieces_kernel(plane, from_near, from_far, *outs):
    for i, out in enumerate(outs):
        out[0] = plane[i * 64 : (i + 1) * 64, :]
        out[1, :32] = from_near[i * 32 : (i + 1) * 32, :]
        out[1, 32:] = from_far[i * 32 : (i + 1) * 32, :]


def place_kernel(my, a, b, c, d, out, slots):
    for i, piece in enumerate((a, b, c, d)):
        slots[2 * i : 2 * i + 2] = piece[...]
    for head in range(8):
        out[:, head * 320 : (head + 1) * 320] = slots[my[SLOT + head]]


def send_back(my, plane, for_near, for_far):
    pieces = call(
        pieces_kernel, [like((2, 64, 320))] * 4, plane, to_near_z(for_near), to_far_z(for_far)
    )
    opposite = to_opposite_x(pieces[3])
    pieces = pieces[0], to_near_x(pieces[1]), to_far_x(pieces[2]), opposite
    return call(
        place_kernel,
        like((64, 2560)),
        my,
        *pieces,
        scalars=1,
        scratch=[pltpu.VMEM((8, 64, 320), BF16)],
    )


def body(tokens, w_qkv, scale_exp, gate_mask, rate, fast_gate, fast_up, fast_down):
    at = lax.axis_index("seq") * 8 + lax.axis_index("head")
    my = lax.dynamic_slice_in_dim(jnp.asarray(table()), at, 1, axis=0).reshape(32)
    tokens, my = lax.optimization_barrier((tokens, my))
    factor = jnp.exp2(scale_exp.astype(F32)).astype(BF16)[:, :, 0]
    factor = jnp.repeat(factor, w_qkv.shape[1] // factor.shape[1], axis=1)[:, None, :]
    w_t = jnp.transpose(w_qkv, (0, 2, 1))
    weight, sent = call(
        weights_kernel,
        [like((1, 384), F32), like((1, 128), F32)],
        my,
        rate,
        gate_mask.reshape(8, 64),
        scalars=2,
    )
    moved = permute(sent, lambda h, y, c, l, x: (h - 1 if l else h + 1, y, c, l, x))
    old_t = [w[0].T for w in (fast_gate, fast_up, fast_down)]
    weff = load(w_t, factor, 1, 2, after=(weight, *old_t))
    plane, others = gather(tokens, (weff,))
    kv1 = project(plane, PLANE, weff, after=others[2:6])
    kv2 = project(others, OTHERS, weff, after=(kv1,))

    grads = (my, kv1, kv2, weight, moved, *old_t)
    sent = call(
        functools.partial(grads_kernel, OTHER_HALF), like((320, 960)), *grads, scalars=1
    )
    got = to_core(sent)
    own = call(
        functools.partial(grads_kernel, OWN_HALF),
        like((320, 960), F32),
        *grads,
        scalars=1,
        after=(sent,),
    )
    to1, to2, to3, mine = call(
        halves_kernel, [like((80, 960))] * 3 + [like((80, 960), F32)], my, own, got, scalars=1
    )
    got = to_y(to2, 2), to_y(to1, 1), to_y(to3, 3)
    weff_q = load(w_t, factor, 0, 1, after=(to1,))
    parts = [like((80, 960), F32), like((40, 960)), like((40, 960))]
    mine, upper, lower = call(sum_kernel, parts, mine, *got, after=(weff_q,))

    got = to_near_h(upper), to_far_h(lower)
    cuts = PLANE + [(len(plane) + i, lo, hi) for i, lo, hi in OTHERS]
    query = project(plane + others, cuts, weff_q, after=(upper,))
    mine, upper, lower = call(pair_kernel, parts, mine, *got, after=(query,))
    got = to_far_h(upper), to_near_h(lower)
    block = call(renorm_kernel, like((80, 960)), my, mine, *got, *old_t, scalars=1)
    column = jnp.concatenate([block, to_y(block, 2), to_y(block, 1), to_y(block, 3)], axis=0)
    other = to_core(column)

    for_near, for_far = call(
        functools.partial(respond_kernel, 256), [like((128, 320))] * 2, query, column, other
    )
    (answers,) = call(
        functools.partial(respond_kernel, 0),
        [like((256, 320))],
        query,
        column,
        other,
        after=(for_near,),
    )
    return send_back(my, answers, for_near, for_far)


def solution(mesh):
    in_specs = (
        P(("seq", "head"), None),
        P(None, None, "head"),
        P(None, None, "head"),
        P("seq", "head"),
        P("head"),
        P("head", None, None),
        P("head", None, None),
        P("head", None, None),
    )
    out_specs = P(("seq", "head"), None)
    return jax.shard_map(body, mesh=mesh, in_specs=in_specs, out_specs=out_specs, check_vma=False)
```

```python
import functools

import jax
import jax.numpy as jnp
import numpy as np
from jax import lax
from jax.experimental import pallas as pl
from jax.experimental.pallas import tpu as pltpu
from jax.sharding import PartitionSpec as P

AXES = ("seq", "head")
BF16 = jnp.bfloat16
F32 = jnp.float32


def place(i):
    seq, head = divmod(i, 8)
    return seq // 8, (seq // 2) % 4, seq % 2, head // 4, head % 4


def permute(value, move):
    pairs = []
    for i in range(256):
        z_hi, y, core, z_lo, x = move(*place(i))
        pairs.append((i, ((z_hi % 4) * 8 + (y % 4) * 2 + core) * 8 + z_lo * 4 + x % 4))
    return lax.ppermute(value, AXES, pairs)


def to_core(value):
    return permute(value, lambda h, y, c, l, x: (h, y, 1 - c, l, x))


def to_y(value, d):
    return permute(value, lambda h, y, c, l, x: (h, y + d, c, l, x))


def to_near_h(value):
    return permute(value, lambda h, y, c, l, x: (near(h), y, c, l, x))


def to_far_h(value):
    return permute(value, lambda h, y, c, l, x: (far(h), y, c, l, x))


def near(x):
    return x ^ 1


def far(x):
    return (x + 1) % 4 if x % 2 else (x - 1) % 4


def to_near_x(value):
    return permute(value, lambda h, y, c, l, x: (h, y, c, l, near(x)))


def to_far_x(value):
    return permute(value, lambda h, y, c, l, x: (h, y, c, l, far(x)))


def to_opposite_x(value):
    return permute(value, lambda h, y, c, l, x: (h, y, c, l, x + 2))


def to_near_z(value):
    return permute(value, lambda h, y, c, l, x: (h, y, c, 1 - l, x))


def to_far_z(value):
    return permute(value, lambda h, y, c, l, x: (h + 1 if l else h - 1, y, c, 1 - l, x))


VMEM = pl.BlockSpec(memory_space=pltpu.VMEM)
SMEM = pl.BlockSpec(memory_space=pltpu.SMEM)
SMALL = pl.CostEstimate(flops=1000, bytes_accessed=1000, transcendentals=0)
PARAMS = pltpu.CompilerParams(vmem_limit_bytes=20 * 1024 * 1024)
BY_ROW = (((1,), (1,)), ((), ()))
BY_TOKEN = (((0,), (0,)), ((), ()))


def like(shape, dtype=BF16):
    return jax.ShapeDtypeStruct(shape, dtype)


def call(kernel, out_shape, *args, scalars=0, after=(), scratch=()):
    n, skip = len(args), len(args) + len(after)

    def run(*refs):
        kernel(*refs[:n], *refs[skip:])

    return pl.pallas_call(
        run,
        out_shape=out_shape,
        in_specs=[SMEM] * scalars + [VMEM] * (n - scalars) + [VMEM] * len(after),
        out_specs=jax.tree.map(lambda _: VMEM, out_shape),
        scratch_shapes=list(scratch),
        compiler_params=PARAMS,
        cost_estimate=SMALL,
    )(*args, *after)


def split_kernel(near_tile, far_tile, z1, z2, near_first, far_second, first, second, both):
    near_first[...] = near_tile[:32, :]
    far_second[...] = far_tile[32:, :]
    first[:16, :] = near_tile[16:32, :]
    first[16:, :] = far_tile[16:32, :]
    second[:16, :] = near_tile[48:, :]
    second[16:, :] = far_tile[48:, :]
    both[:16, :] = z1[:16, :]
    both[16:, :] = z2[:16, :]


def load_kernel(first, w_hbm, f_ref, out, sems):
    copies = []
    for c in range(out.shape[0]):
        for i in range(4):
            at = pl.ds(i * 80, 80)
            source, target = w_hbm.at[first + c, at, :], out.at[c, at, :]
            copies.append((c, at, pltpu.make_async_copy(source, target, sems.at[c * 4 + i])))
    for _, _, copy in copies:
        copy.start()
    for c, at, copy in copies:
        copy.wait()
        out[c, at, :] = out[c, at, :] * f_ref[first + c]


def load(w_t, factor, first, count, after=()):
    def run(*refs):
        load_kernel(first, *refs[:2], *refs[-2:])

    return pl.pallas_call(
        run,
        out_shape=like((count, *w_t.shape[1:])),
        in_specs=[pl.BlockSpec(memory_space=pl.ANY), VMEM] + [VMEM] * len(after),
        out_specs=VMEM,
        scratch_shapes=[pltpu.SemaphoreType.DMA((count * 4,))],
        compiler_params=pltpu.CompilerParams(vmem_limit_bytes=44 * 1024 * 1024),
        cost_estimate=SMALL,
    )(w_t, factor, *after)


def project_kernel(cuts, *refs):
    tiles, (w_ref, out) = refs[:-2], refs[-2:]
    tile = jnp.concatenate([tiles[i][lo:hi, :] for i, lo, hi in cuts], axis=0)
    for c in range(w_ref.shape[0]):
        part = lax.dot_general(w_ref[c], tile, BY_ROW, preferred_element_type=F32)
        out[c * 320 : (c + 1) * 320, :] = part.astype(BF16)


def project(tiles, cuts, weff, after=()):
    shape = (weff.shape[0] * weff.shape[1], sum(hi - lo for _, lo, hi in cuts))
    return call(functools.partial(project_kernel, cuts), like(shape), *tiles, weff, after=after)


def grads_kernel(which, my, kv1, kv2, weight, moved, gate_t, up_t, down_t, out):
    half = pl.ds(pl.multiple_of(my[which], 16), 320)
    weight = jnp.concatenate([weight[...], moved[...]], axis=1)
    keys = jnp.concatenate([kv1[:320, :], kv2[:320, :]], axis=1)
    values = jnp.concatenate([kv1[320:, :], kv2[320:, :]], axis=1)
    gate = jnp.dot(gate_t[half, :], keys, preferred_element_type=F32)
    upper = jnp.dot(up_t[half, :], keys, preferred_element_type=F32)
    sigma = jax.nn.sigmoid(gate)
    active = gate * sigma
    hidden = (active * upper).astype(BF16)
    weighted = (weight * values.astype(F32)).astype(BF16)
    d_hidden = jnp.dot(down_t[half, :], weighted, preferred_element_type=F32)
    d_gate = (d_hidden * upper * sigma * (1.0 + gate * (1.0 - sigma))).astype(BF16)
    d_upper = (d_hidden * active).astype(BF16)
    pairs = ((d_gate, keys), (d_upper, keys), (hidden, weighted))
    for i, (left, right) in enumerate(pairs):
        grad = lax.dot_general(left, right, BY_ROW, preferred_element_type=F32)
        out[:, i * 320 : (i + 1) * 320] = grad.astype(out.dtype)


def halves_kernel(my, own, got, to1, to2, to3, mine):
    for d, out in ((1, to1), (2, to2), (3, to3), (0, mine)):
        at = pl.ds(pl.multiple_of(lax.rem(my[Y] + d, 4) * 80, 16), 80)
        out[...] = (own[at, :] + got[at, :].astype(F32)).astype(out.dtype)


def sum_kernel(mine, a, b, c, total, upper, lower):
    result = mine[...] + a[...].astype(F32) + b[...].astype(F32) + c[...].astype(F32)
    total[...] = result
    upper[...] = result[:40].astype(BF16)
    lower[...] = result[40:].astype(BF16)


def pair_kernel(mine, a, b, total, upper, lower):
    total[:40, :] = mine[:40, :] + a[...].astype(F32)
    total[40:, :] = mine[40:, :] + b[...].astype(F32)
    upper[...] = total[:40, :].astype(BF16)
    lower[...] = total[40:, :].astype(BF16)


def renorm_kernel(my, mine, a, b, gate_t, up_t, down_t, out):
    got = jnp.concatenate([a[...].astype(F32), b[...].astype(F32)], axis=0)
    total = mine[...] + got
    mine_rows = pl.ds(pl.multiple_of(my[BLOCK], 16), 80)
    for i, old in enumerate((gate_t, up_t, down_t)):
        at = slice(i * 320, (i + 1) * 320)
        before = old[mine_rows, :].astype(F32)
        fresh = before + total[:, at]
        old_norm = jnp.sqrt(jnp.sum(before * before, axis=1, keepdims=True))
        new_sq = jnp.sum(fresh * fresh, axis=1, keepdims=True)
        out[:, at] = (fresh * (old_norm / jnp.sqrt(new_sq + 1e-06))).astype(BF16)


def respond_kernel(start, query_ref, *refs):
    blocks, outs = refs[:8], refs[8:]
    renorm = jnp.concatenate([block[...] for block in blocks], axis=0)
    query = query_ref[:, start : start + 256]
    gate = jnp.dot(renorm[:, :320], query, preferred_element_type=F32)
    upper = jnp.dot(renorm[:, 320:640], query, preferred_element_type=F32)
    hidden = (gate * jax.nn.sigmoid(gate) * upper).astype(BF16)
    output = lax.dot_general(hidden, renorm[:, 640:], BY_TOKEN, preferred_element_type=F32)
    scaled = output * lax.rsqrt(jnp.mean(output * output, axis=-1, keepdims=True) + 1e-05)
    answer = scaled.astype(BF16)
    at = 0
    for out in outs:
        n = out.shape[0]
        out[:, :320] = answer[at : at + n]
        out[:, 320:] = answer[at + n : at + 2 * n]
        at += 2 * n


PLANE = [(0, 0, 64), (1, 0, 64), (2, 0, 64), (3, 0, 32), (4, 0, 32)]
OTHERS = [(0, 0, 32), (2, 0, 16), (4, 0, 16), (3, 0, 16), (4, 16, 32), (6, 0, 32)]
OTHERS += [(1, 0, 32), (2, 16, 32), (5, 0, 16), (3, 16, 32), (5, 16, 32), (7, 0, 32)]


def gather(tokens, work):
    near_tile, far_tile = to_near_x(tokens), to_far_x(tokens)
    z1, z2 = to_near_z(tokens[:32]), to_far_z(tokens[32:])
    near_first, far_second, first, second, both = call(
        split_kernel, [like((32, 5120))] * 5, near_tile, far_tile, z1, z2, after=work
    )
    opposite_first, opposite_second = to_far_x(near_first), to_near_x(far_second)
    z3, z4 = to_near_z(first), to_far_z(second)
    near_both, far_both = to_near_x(both), to_far_x(both)
    z5, z6 = to_near_z(opposite_first), to_far_z(opposite_second)
    return (
        [tokens, near_tile, far_tile, opposite_first, opposite_second],
        [z1, z2, near_both, far_both, z3, z4, z5, z6],
    )


OWN_HALF, OTHER_HALF, Y, BLOCK, SAME, OTHER, SLOT = 0, 1, 2, 3, 4, 8, 12


def table():
    lines = np.zeros((256, 32), np.int32)
    for i in range(256):
        _, y, core, z_lo, x = place(i)
        order = [x, near(x), far(x), (x + 2) % 4]
        lines[i, :4] = core * 320, 320 - core * 320, y, core * 320 + y * 80
        lines[i, SAME : SAME + 4] = [z_lo * 4 + t for t in order]
        lines[i, OTHER : OTHER + 4] = [(1 - z_lo) * 4 + t for t in order]
        lines[i, SLOT : SLOT + 8] = [order.index(h % 4) * 2 + (h // 4 != z_lo) for h in range(8)]
    return lines


def weights_kernel(my, rate, mask, weight, sent):
    for i in range(4):
        same = mask[pl.ds(my[SAME + i], 1), :].astype(F32) * rate[0]
        other = mask[pl.ds(my[OTHER + i], 1), :].astype(F32) * rate[0]
        weight[:, i * 64 : (i + 1) * 64] = same
        weight[:, 256 + i * 32 : 288 + i * 32] = other[:, :32]
        sent[:, i * 32 : (i + 1) * 32] = other[:, 32:]


def pieces_kernel(from_near, from_far, *outs):
    for i, out in enumerate(outs):
        at = slice(i % 2 * 32, i % 2 * 32 + 32), slice(i // 2 * 320, i // 2 * 320 + 320)
        out[:, :320] = from_near[at]
        out[:, 320:] = from_far[at]


def place_kernel(my, *refs):
    pieces, out, slots = refs[:8], refs[8], refs[9]
    for i, piece in enumerate(pieces):
        slots[i, :32] = piece[:, :320]
        slots[i, 32:] = piece[:, 320:]
    for head in range(8):
        out[:, head * 320 : (head + 1) * 320] = slots[my[SLOT + head]]


def to_plane(pieces):
    opposite, near_piece = to_opposite_x(pieces[3]), to_near_x(pieces[1])
    return pieces[0], near_piece, to_far_x(pieces[2]), opposite


def send_back(my, plane, for_near, for_far):
    from_near, from_far = to_near_z(for_near), to_far_z(for_far)
    own = to_plane(plane)
    pieces = call(pieces_kernel, [like((32, 640))] * 4, from_near, from_far, after=own[1:])
    other = to_plane(pieces)
    slots = [piece for pair in zip(own, other) for piece in pair]
    return call(
        place_kernel,
        like((64, 2560)),
        my,
        *slots,
        scalars=1,
        scratch=[pltpu.VMEM((8, 64, 320), BF16)],
    )


def body(tokens, w_qkv, scale_exp, gate_mask, rate, fast_gate, fast_up, fast_down):
    at = lax.axis_index("seq") * 8 + lax.axis_index("head")
    my = lax.dynamic_slice_in_dim(jnp.asarray(table()), at, 1, axis=0).reshape(32)
    tokens, my = lax.optimization_barrier((tokens, my))
    factor = jnp.exp2(scale_exp.astype(F32)).astype(BF16)[:, :, 0]
    factor = jnp.repeat(factor, w_qkv.shape[1] // factor.shape[1], axis=1)[:, None, :]
    w_t = jnp.transpose(w_qkv, (0, 2, 1))
    weight, sent = call(
        weights_kernel,
        [like((1, 384), F32), like((1, 128), F32)],
        my,
        rate,
        gate_mask.reshape(8, 64),
        scalars=2,
    )
    moved = permute(sent, lambda h, y, c, l, x: (h - 1 if l else h + 1, y, c, l, x))
    old_t = [w[0].T for w in (fast_gate, fast_up, fast_down)]
    weff = load(w_t, factor, 1, 2, after=(weight, *old_t))
    plane, others = gather(tokens, (weff,))
    kv1 = project(plane, PLANE, weff, after=others[2:6])
    kv2 = project(others, OTHERS, weff, after=(kv1,))

    grads = (my, kv1, kv2, weight, moved, *old_t)
    sent = call(
        functools.partial(grads_kernel, OTHER_HALF), like((320, 960)), *grads, scalars=1
    )
    got = to_core(sent)
    own = call(
        functools.partial(grads_kernel, OWN_HALF),
        like((320, 960), F32),
        *grads,
        scalars=1,
        after=(sent,),
    )
    to1, to2, to3, mine = call(
        halves_kernel, [like((80, 960))] * 3 + [like((80, 960), F32)], my, own, got, scalars=1
    )
    got = to_y(to2, 2), to_y(to1, 1), to_y(to3, 3)
    weff_q = load(w_t, factor, 0, 1, after=(to1,))
    parts = [like((80, 960), F32), like((40, 960)), like((40, 960))]
    mine, upper, lower = call(sum_kernel, parts, mine, *got, after=(weff_q,))

    got = to_near_h(upper), to_far_h(lower)
    cuts = PLANE + [(len(plane) + i, lo, hi) for i, lo, hi in OTHERS]
    query = project(plane + others, cuts, weff_q, after=(upper,))
    mine, upper, lower = call(pair_kernel, parts, mine, *got, after=(query,))
    got = to_far_h(upper), to_near_h(lower)
    block = call(renorm_kernel, like((80, 960)), my, mine, *got, *old_t, scalars=1)
    column = [block, to_y(block, 1), to_y(block, 3), to_y(block, 2)]
    blocks = column + [to_core(b) for b in column]

    for_near, for_far = call(
        functools.partial(respond_kernel, 256), [like((64, 640))] * 2, query, *blocks
    )
    plane = call(
        functools.partial(respond_kernel, 0),
        [like((32, 640))] * 4,
        query,
        *blocks,
        after=(for_near,),
    )
    return send_back(my, plane, for_near, for_far)


def solution(mesh):
    in_specs = (
        P(("seq", "head"), None),
        P(None, None, "head"),
        P(None, None, "head"),
        P("seq", "head"),
        P("head"),
        P("head", None, None),
        P("head", None, None),
        P("head", None, None),
    )
    out_specs = P(("seq", "head"), None)
    return jax.shard_map(body, mesh=mesh, in_specs=in_specs, out_specs=out_specs, check_vma=False)
```

```python
import functools

import jax
import jax.numpy as jnp
import numpy as np
from jax import lax
from jax.experimental import pallas as pl
from jax.experimental.pallas import tpu as pltpu
from jax.sharding import PartitionSpec as P

AXES = ("seq", "head")
BF16 = jnp.bfloat16
F32 = jnp.float32


def place(i):
    seq, head = divmod(i, 8)
    return seq // 8, (seq // 2) % 4, seq % 2, head // 4, head % 4


def permute(value, move):
    pairs = []
    for i in range(256):
        z_hi, y, core, z_lo, x = move(*place(i))
        pairs.append((i, ((z_hi % 4) * 8 + (y % 4) * 2 + core) * 8 + z_lo * 4 + x % 4))
    return lax.ppermute(value, AXES, pairs)


def to_core(value):
    return permute(value, lambda h, y, c, l, x: (h, y, 1 - c, l, x))


def to_y(value, d):
    return permute(value, lambda h, y, c, l, x: (h, y + d, c, l, x))


def to_near_h(value):
    return permute(value, lambda h, y, c, l, x: (near(h), y, c, l, x))


def to_far_h(value):
    return permute(value, lambda h, y, c, l, x: (far(h), y, c, l, x))


def near(x):
    return x ^ 1


def far(x):
    return (x + 1) % 4 if x % 2 else (x - 1) % 4


def to_near_x(value):
    return permute(value, lambda h, y, c, l, x: (h, y, c, l, near(x)))


def to_far_x(value):
    return permute(value, lambda h, y, c, l, x: (h, y, c, l, far(x)))


def to_opposite_x(value):
    return permute(value, lambda h, y, c, l, x: (h, y, c, l, x + 2))


def to_near_z(value):
    return permute(value, lambda h, y, c, l, x: (h, y, c, 1 - l, x))


def to_far_z(value):
    return permute(value, lambda h, y, c, l, x: (h + 1 if l else h - 1, y, c, 1 - l, x))


VMEM = pl.BlockSpec(memory_space=pltpu.VMEM)
SMEM = pl.BlockSpec(memory_space=pltpu.SMEM)
SMALL = pl.CostEstimate(flops=1000, bytes_accessed=1000, transcendentals=0)
PARAMS = pltpu.CompilerParams(vmem_limit_bytes=20 * 1024 * 1024)
BY_ROW = (((1,), (1,)), ((), ()))
BY_TOKEN = (((0,), (0,)), ((), ()))


def like(shape, dtype=BF16):
    return jax.ShapeDtypeStruct(shape, dtype)


def call(kernel, out_shape, *args, scalars=0, after=(), scratch=()):
    n, skip = len(args), len(args) + len(after)

    def run(*refs):
        kernel(*refs[:n], *refs[skip:])

    return pl.pallas_call(
        run,
        out_shape=out_shape,
        in_specs=[SMEM] * scalars + [VMEM] * (n - scalars) + [VMEM] * len(after),
        out_specs=jax.tree.map(lambda _: VMEM, out_shape),
        scratch_shapes=list(scratch),
        compiler_params=PARAMS,
        cost_estimate=SMALL,
    )(*args, *after)


def halve_kernel(tile, first, second):
    first[...] = tile[:32, :]
    second[...] = tile[32:, :]


def split_kernel(near_a, near_b, far_a, far_b, z1, z2, first, second, both):
    first[:16, :] = near_a[16:, :]
    first[16:, :] = far_a[16:, :]
    second[:16, :] = near_b[16:, :]
    second[16:, :] = far_b[16:, :]
    both[:16, :] = z1[:16, :]
    both[16:, :] = z2[:16, :]


def load_kernel(first, w_hbm, f_ref, out, sems):
    copies = []
    for c in range(out.shape[0]):
        for i in range(4):
            at = pl.ds(i * 80, 80)
            source, target = w_hbm.at[first + c, at, :], out.at[c, at, :]
            copies.append((c, at, pltpu.make_async_copy(source, target, sems.at[c * 4 + i])))
    for _, _, copy in copies:
        copy.start()
    for c, at, copy in copies:
        copy.wait()
        out[c, at, :] = out[c, at, :] * f_ref[first + c]


def load(w_t, factor, first, count, after=()):
    def run(*refs):
        load_kernel(first, *refs[:2], *refs[-2:])

    return pl.pallas_call(
        run,
        out_shape=like((count, *w_t.shape[1:])),
        in_specs=[pl.BlockSpec(memory_space=pl.ANY), VMEM] + [VMEM] * len(after),
        out_specs=VMEM,
        scratch_shapes=[pltpu.SemaphoreType.DMA((count * 4,))],
        compiler_params=pltpu.CompilerParams(vmem_limit_bytes=44 * 1024 * 1024),
        cost_estimate=SMALL,
    )(w_t, factor, *after)


def project_kernel(cuts, *refs):
    tiles, (w_ref, out) = refs[:-2], refs[-2:]
    tile = jnp.concatenate([tiles[i][lo:hi, :] for i, lo, hi in cuts], axis=0)
    for c in range(w_ref.shape[0]):
        part = lax.dot_general(w_ref[c], tile, BY_ROW, preferred_element_type=F32)
        out[c * 320 : (c + 1) * 320, :] = part.astype(BF16)


def project(tiles, cuts, weff, after=()):
    shape = (weff.shape[0] * weff.shape[1], sum(hi - lo for _, lo, hi in cuts))
    return call(functools.partial(project_kernel, cuts), like(shape), *tiles, weff, after=after)


def grads_kernel(which, my, kv1, kv2, weight, moved, gate_t, up_t, down_t, out):
    half = pl.ds(pl.multiple_of(my[which], 16), 320)
    weight = jnp.concatenate([weight[...], moved[...]], axis=1)
    keys = jnp.concatenate([kv1[:320, :], kv2[:320, :]], axis=1)
    values = jnp.concatenate([kv1[320:, :], kv2[320:, :]], axis=1)
    gate = jnp.dot(gate_t[half, :], keys, preferred_element_type=F32)
    upper = jnp.dot(up_t[half, :], keys, preferred_element_type=F32)
    sigma = jax.nn.sigmoid(gate)
    active = gate * sigma
    hidden = (active * upper).astype(BF16)
    weighted = (weight * values.astype(F32)).astype(BF16)
    d_hidden = jnp.dot(down_t[half, :], weighted, preferred_element_type=F32)
    d_gate = (d_hidden * upper * sigma * (1.0 + gate * (1.0 - sigma))).astype(BF16)
    d_upper = (d_hidden * active).astype(BF16)
    pairs = ((d_gate, keys), (d_upper, keys), (hidden, weighted))
    for i, (left, right) in enumerate(pairs):
        grad = lax.dot_general(left, right, BY_ROW, preferred_element_type=F32)
        out[:, i * 320 : (i + 1) * 320] = grad.astype(out.dtype)


def halves_kernel(my, own, got, to1, to2, to3, mine):
    for d, out in ((1, to1), (2, to2), (3, to3), (0, mine)):
        at = pl.ds(pl.multiple_of(lax.rem(my[Y] + d, 4) * 80, 16), 80)
        out[...] = (own[at, :] + got[at, :].astype(F32)).astype(out.dtype)


def sum_kernel(mine, a, b, c, total, upper, lower):
    result = mine[...] + a[...].astype(F32) + b[...].astype(F32) + c[...].astype(F32)
    total[...] = result
    upper[...] = result[:40].astype(BF16)
    lower[...] = result[40:].astype(BF16)


def pair_kernel(mine, a, b, total, upper, lower):
    total[:40, :] = mine[:40, :] + a[...].astype(F32)
    total[40:, :] = mine[40:, :] + b[...].astype(F32)
    upper[...] = total[:40, :].astype(BF16)
    lower[...] = total[40:, :].astype(BF16)


def renorm_kernel(my, mine, a, b, gate_t, up_t, down_t, out):
    got = jnp.concatenate([a[...].astype(F32), b[...].astype(F32)], axis=0)
    total = mine[...] + got
    mine_rows = pl.ds(pl.multiple_of(my[BLOCK], 16), 80)
    for i, old in enumerate((gate_t, up_t, down_t)):
        at = slice(i * 320, (i + 1) * 320)
        before = old[mine_rows, :].astype(F32)
        fresh = before + total[:, at]
        old_norm = jnp.sqrt(jnp.sum(before * before, axis=1, keepdims=True))
        new_sq = jnp.sum(fresh * fresh, axis=1, keepdims=True)
        out[:, at] = (fresh * (old_norm / jnp.sqrt(new_sq + 1e-06))).astype(BF16)


def respond_kernel(start, query_ref, *refs):
    blocks, outs = refs[:8], refs[8:]
    renorm = jnp.concatenate([block[...] for block in blocks], axis=0)
    query = query_ref[:, start : start + 256]
    gate = jnp.dot(renorm[:, :320], query, preferred_element_type=F32)
    upper = jnp.dot(renorm[:, 320:640], query, preferred_element_type=F32)
    hidden = (gate * jax.nn.sigmoid(gate) * upper).astype(BF16)
    output = lax.dot_general(hidden, renorm[:, 640:], BY_TOKEN, preferred_element_type=F32)
    scaled = output * lax.rsqrt(jnp.mean(output * output, axis=-1, keepdims=True) + 1e-05)
    answer = scaled.astype(BF16)
    at = 0
    for out in outs:
        n = out.shape[0]
        out[:, :320] = answer[at : at + n]
        out[:, 320:] = answer[at + n : at + 2 * n]
        at += 2 * n


PLANE = [(0, 0, 64)] + [(i, 0, 32) for i in range(1, 7)]
OTHERS = [(0, 0, 32), (2, 0, 16), (4, 0, 16), (3, 0, 16), (4, 16, 32), (6, 0, 32)]
OTHERS += [(1, 0, 32), (2, 16, 32), (5, 0, 16), (3, 16, 32), (5, 16, 32), (7, 0, 32)]


def gather(tokens, work):
    half = [like((32, 5120))]
    a, b = call(halve_kernel, half * 2, tokens)
    near_a, far_b = to_near_x(a), to_far_x(b)
    z1, z2 = to_near_z(a), to_far_z(b)
    near_b, far_a = to_near_x(b), to_far_x(a)
    opposite_first, opposite_second = to_far_x(near_a), to_near_x(far_b)
    first, second, both = call(
        split_kernel, half * 3, near_a, near_b, far_a, far_b, z1, z2, after=work
    )
    z3, z4 = to_near_z(first), to_far_z(second)
    near_both, far_both = to_near_x(both), to_far_x(both)
    z5, z6 = to_near_z(opposite_first), to_far_z(opposite_second)
    return (
        [tokens, near_a, near_b, far_a, far_b, opposite_first, opposite_second],
        [z1, z2, near_both, far_both, z3, z4, z5, z6],
    )


OWN_HALF, OTHER_HALF, Y, BLOCK, SAME, OTHER, SLOT = 0, 1, 2, 3, 4, 8, 12


def table():
    lines = np.zeros((256, 32), np.int32)
    for i in range(256):
        _, y, core, z_lo, x = place(i)
        order = [x, near(x), far(x), (x + 2) % 4]
        lines[i, :4] = core * 320, 320 - core * 320, y, core * 320 + y * 80
        lines[i, SAME : SAME + 4] = [z_lo * 4 + t for t in order]
        lines[i, OTHER : OTHER + 4] = [(1 - z_lo) * 4 + t for t in order]
        lines[i, SLOT : SLOT + 8] = [order.index(h % 4) * 2 + (h // 4 != z_lo) for h in range(8)]
    return lines


def weights_kernel(my, rate, mask, weight, sent):
    for i in range(4):
        same = mask[pl.ds(my[SAME + i], 1), :].astype(F32) * rate[0]
        other = mask[pl.ds(my[OTHER + i], 1), :].astype(F32) * rate[0]
        weight[:, i * 64 : (i + 1) * 64] = same
        weight[:, 256 + i * 32 : 288 + i * 32] = other[:, :32]
        sent[:, i * 32 : (i + 1) * 32] = other[:, 32:]


def pieces_kernel(plane, from_near, from_far, *outs):
    for i, out in enumerate(outs):
        run = slice(i // 2 * 320, i // 2 * 320 + 320)
        half = slice(i % 2 * 32, i % 2 * 32 + 32)
        out[:, :320] = plane[i % 2 * 64 : i % 2 * 64 + 64, run]
        out[:32, 320:] = from_near[half, run]
        out[32:, 320:] = from_far[half, run]


def place_kernel(my, a, b, c, d, out, slots):
    for i, piece in enumerate((a, b, c, d)):
        slots[2 * i] = piece[:, :320]
        slots[2 * i + 1] = piece[:, 320:]
    for head in range(8):
        out[:, head * 320 : (head + 1) * 320] = slots[my[SLOT + head]]


def send_back(my, plane, for_near, for_far):
    pieces = call(
        pieces_kernel, [like((64, 640))] * 4, plane, to_near_z(for_near), to_far_z(for_far)
    )
    opposite = to_opposite_x(pieces[3])
    pieces = pieces[0], to_near_x(pieces[1]), to_far_x(pieces[2]), opposite
    return call(
        place_kernel,
        like((64, 2560)),
        my,
        *pieces,
        scalars=1,
        scratch=[pltpu.VMEM((8, 64, 320), BF16)],
    )


def body(tokens, w_qkv, scale_exp, gate_mask, rate, fast_gate, fast_up, fast_down):
    at = lax.axis_index("seq") * 8 + lax.axis_index("head")
    my = lax.dynamic_slice_in_dim(jnp.asarray(table()), at, 1, axis=0).reshape(32)
    tokens, my = lax.optimization_barrier((tokens, my))
    factor = jnp.exp2(scale_exp.astype(F32)).astype(BF16)[:, :, 0]
    factor = jnp.repeat(factor, w_qkv.shape[1] // factor.shape[1], axis=1)[:, None, :]
    w_t = jnp.transpose(w_qkv, (0, 2, 1))
    weight, sent = call(
        weights_kernel,
        [like((1, 384), F32), like((1, 128), F32)],
        my,
        rate,
        gate_mask.reshape(8, 64),
        scalars=2,
    )
    moved = permute(sent, lambda h, y, c, l, x: (h - 1 if l else h + 1, y, c, l, x))
    old_t = [w[0].T for w in (fast_gate, fast_up, fast_down)]
    weff = load(w_t, factor, 1, 2, after=(weight, *old_t))
    plane, others = gather(tokens, (weff,))
    kv1 = project(plane, PLANE, weff, after=others[2:6])
    kv2 = project(others, OTHERS, weff, after=(kv1,))

    grads = (my, kv1, kv2, weight, moved, *old_t)
    sent = call(
        functools.partial(grads_kernel, OTHER_HALF), like((320, 960)), *grads, scalars=1
    )
    got = to_core(sent)
    own = call(
        functools.partial(grads_kernel, OWN_HALF),
        like((320, 960), F32),
        *grads,
        scalars=1,
        after=(sent,),
    )
    to1, to2, to3, mine = call(
        halves_kernel, [like((80, 960))] * 3 + [like((80, 960), F32)], my, own, got, scalars=1
    )
    got = to_y(to2, 2), to_y(to1, 1), to_y(to3, 3)
    weff_q = load(w_t, factor, 0, 1, after=(to1,))
    parts = [like((80, 960), F32), like((40, 960)), like((40, 960))]
    mine, upper, lower = call(sum_kernel, parts, mine, *got, after=(weff_q,))

    got = to_near_h(upper), to_far_h(lower)
    cuts = PLANE + [(len(plane) + i, lo, hi) for i, lo, hi in OTHERS]
    query = project(plane + others, cuts, weff_q, after=(upper,))
    mine, upper, lower = call(pair_kernel, parts, mine, *got, after=(query,))
    got = to_far_h(upper), to_near_h(lower)
    block = call(renorm_kernel, like((80, 960)), my, mine, *got, *old_t, scalars=1)
    column = [block, to_y(block, 1), to_y(block, 3), to_y(block, 2)]
    blocks = column + [to_core(b) for b in column]

    for_near, for_far = call(
        functools.partial(respond_kernel, 256), [like((64, 640))] * 2, query, *blocks
    )
    (plane,) = call(
        functools.partial(respond_kernel, 0),
        [like((128, 640))],
        query,
        *blocks,
        after=(for_near,),
    )
    return send_back(my, plane, for_near, for_far)


def solution(mesh):
    in_specs = (
        P(("seq", "head"), None),
        P(None, None, "head"),
        P(None, None, "head"),
        P("seq", "head"),
        P("head"),
        P("head", None, None),
        P("head", None, None),
        P("head", None, None),
    )
    out_specs = P(("seq", "head"), None)
    return jax.shard_map(body, mesh=mesh, in_specs=in_specs, out_specs=out_specs, check_vma=False)
```

```python
import functools

import jax
import jax.numpy as jnp
import numpy as np
from jax import lax
from jax.experimental import pallas as pl
from jax.experimental.pallas import tpu as pltpu
from jax.sharding import PartitionSpec as P

AXES = ("seq", "head")
BF16 = jnp.bfloat16
F32 = jnp.float32


def place(i):
    seq, head = divmod(i, 8)
    return seq // 8, (seq // 2) % 4, seq % 2, head // 4, head % 4


def permute(value, move):
    pairs = []
    for i in range(256):
        z_hi, y, core, z_lo, x = move(*place(i))
        pairs.append((i, ((z_hi % 4) * 8 + (y % 4) * 2 + core) * 8 + z_lo * 4 + x % 4))
    return lax.ppermute(value, AXES, pairs)


def to_core(value):
    return permute(value, lambda h, y, c, l, x: (h, y, 1 - c, l, x))


def to_y(value, d):
    return permute(value, lambda h, y, c, l, x: (h, y + d, c, l, x))


def to_near_h(value):
    return permute(value, lambda h, y, c, l, x: (near(h), y, c, l, x))


def to_far_h(value):
    return permute(value, lambda h, y, c, l, x: (far(h), y, c, l, x))


def near(x):
    return x ^ 1


def far(x):
    return (x + 1) % 4 if x % 2 else (x - 1) % 4


def to_near_x(value):
    return permute(value, lambda h, y, c, l, x: (h, y, c, l, near(x)))


def to_far_x(value):
    return permute(value, lambda h, y, c, l, x: (h, y, c, l, far(x)))


def to_opposite_x(value):
    return permute(value, lambda h, y, c, l, x: (h, y, c, l, x + 2))


def to_near_z(value):
    return permute(value, lambda h, y, c, l, x: (h, y, c, 1 - l, x))


def to_far_z(value):
    return permute(value, lambda h, y, c, l, x: (h + 1 if l else h - 1, y, c, 1 - l, x))


VMEM = pl.BlockSpec(memory_space=pltpu.VMEM)
SMEM = pl.BlockSpec(memory_space=pltpu.SMEM)
SMALL = pl.CostEstimate(flops=1000, bytes_accessed=1000, transcendentals=0)
PARAMS = pltpu.CompilerParams(vmem_limit_bytes=20 * 1024 * 1024)
BY_ROW = (((1,), (1,)), ((), ()))
BY_TOKEN = (((0,), (0,)), ((), ()))


def like(shape, dtype=BF16):
    return jax.ShapeDtypeStruct(shape, dtype)


def call(kernel, out_shape, *args, scalars=0, after=(), scratch=()):
    n, skip = len(args), len(args) + len(after)

    def run(*refs):
        kernel(*refs[:n], *refs[skip:])

    return pl.pallas_call(
        run,
        out_shape=out_shape,
        in_specs=[SMEM] * scalars + [VMEM] * (n - scalars) + [VMEM] * len(after),
        out_specs=jax.tree.map(lambda _: VMEM, out_shape),
        scratch_shapes=list(scratch),
        compiler_params=PARAMS,
        cost_estimate=SMALL,
    )(*args, *after)


def split_kernel(near_tile, far_tile, z1, z2, near_first, far_second, first, second, both):
    near_first[...] = near_tile[:32, :]
    far_second[...] = far_tile[32:, :]
    first[:16, :] = near_tile[16:32, :]
    first[16:, :] = far_tile[16:32, :]
    second[:16, :] = near_tile[48:, :]
    second[16:, :] = far_tile[48:, :]
    both[:16, :] = z1[:16, :]
    both[16:, :] = z2[:16, :]


def load_kernel(first, w_hbm, f_ref, out, sems):
    copies = []
    for c in range(out.shape[0]):
        for i in range(4):
            at = pl.ds(i * 80, 80)
            source, target = w_hbm.at[first + c, at, :], out.at[c, at, :]
            copies.append((c, at, pltpu.make_async_copy(source, target, sems.at[c * 4 + i])))
    for _, _, copy in copies:
        copy.start()
    for c, at, copy in copies:
        copy.wait()
        out[c, at, :] = out[c, at, :] * f_ref[first + c]


def load(w_t, factor, first, count, after=()):
    def run(*refs):
        load_kernel(first, *refs[:2], *refs[-2:])

    return pl.pallas_call(
        run,
        out_shape=like((count, *w_t.shape[1:])),
        in_specs=[pl.BlockSpec(memory_space=pl.ANY), VMEM] + [VMEM] * len(after),
        out_specs=VMEM,
        scratch_shapes=[pltpu.SemaphoreType.DMA((count * 4,))],
        compiler_params=pltpu.CompilerParams(vmem_limit_bytes=44 * 1024 * 1024),
        cost_estimate=SMALL,
    )(w_t, factor, *after)


def project_kernel(cuts, *refs):
    tiles, (w_ref, out) = refs[:-2], refs[-2:]
    tile = jnp.concatenate([tiles[i][lo:hi, :] for i, lo, hi in cuts], axis=0)
    for c in range(w_ref.shape[0]):
        part = lax.dot_general(w_ref[c], tile, BY_ROW, preferred_element_type=F32)
        out[c * 320 : (c + 1) * 320, :] = part.astype(BF16)


def project(tiles, cuts, weff, after=()):
    shape = (weff.shape[0] * weff.shape[1], sum(hi - lo for _, lo, hi in cuts))
    return call(functools.partial(project_kernel, cuts), like(shape), *tiles, weff, after=after)


def grads_kernel(which, my, kv1, kv2, weight, moved, gate_t, up_t, down_t, out):
    half = pl.ds(pl.multiple_of(my[which], 16), 320)
    weight = jnp.concatenate([weight[...], moved[...]], axis=1)
    keys = jnp.concatenate([kv1[:320, :], kv2[:320, :]], axis=1)
    values = jnp.concatenate([kv1[320:, :], kv2[320:, :]], axis=1)
    gate = jnp.dot(gate_t[half, :], keys, preferred_element_type=F32)
    upper = jnp.dot(up_t[half, :], keys, preferred_element_type=F32)
    sigma = jax.nn.sigmoid(gate)
    active = gate * sigma
    hidden = (active * upper).astype(BF16)
    weighted = (weight * values.astype(F32)).astype(BF16)
    d_hidden = jnp.dot(down_t[half, :], weighted, preferred_element_type=F32)
    d_gate = (d_hidden * upper * sigma * (1.0 + gate * (1.0 - sigma))).astype(BF16)
    d_upper = (d_hidden * active).astype(BF16)
    pairs = ((d_gate, keys), (d_upper, keys), (hidden, weighted))
    for i, (left, right) in enumerate(pairs):
        grad = lax.dot_general(left, right, BY_ROW, preferred_element_type=F32)
        out[:, i * 320 : (i + 1) * 320] = grad.astype(out.dtype)


def halves_kernel(my, own, got, to1, to2, to3, mine):
    for d, out in ((1, to1), (2, to2), (3, to3), (0, mine)):
        at = pl.ds(pl.multiple_of(lax.rem(my[Y] + d, 4) * 80, 16), 80)
        out[...] = (own[at, :] + got[at, :].astype(F32)).astype(out.dtype)


def sum_kernel(mine, a, b, c, total, upper, lower):
    result = mine[...] + a[...].astype(F32) + b[...].astype(F32) + c[...].astype(F32)
    total[...] = result
    upper[...] = result[:40].astype(BF16)
    lower[...] = result[40:].astype(BF16)


def pair_kernel(mine, a, b, total, upper, lower):
    total[:40, :] = mine[:40, :] + a[...].astype(F32)
    total[40:, :] = mine[40:, :] + b[...].astype(F32)
    upper[...] = total[:40, :].astype(BF16)
    lower[...] = total[40:, :].astype(BF16)


def renorm_kernel(my, mine, a, b, gate_t, up_t, down_t, out):
    got = jnp.concatenate([a[...].astype(F32), b[...].astype(F32)], axis=0)
    total = mine[...] + got
    mine_rows = pl.ds(pl.multiple_of(my[BLOCK], 16), 80)
    for i, old in enumerate((gate_t, up_t, down_t)):
        at = slice(i * 320, (i + 1) * 320)
        before = old[mine_rows, :].astype(F32)
        fresh = before + total[:, at]
        old_norm = jnp.sqrt(jnp.sum(before * before, axis=1, keepdims=True))
        new_sq = jnp.sum(fresh * fresh, axis=1, keepdims=True)
        out[:, at] = (fresh * (old_norm / jnp.sqrt(new_sq + 1e-06))).astype(BF16)


def respond_kernel(start, query_ref, *refs):
    blocks, outs = refs[:8], refs[8:]
    renorm = jnp.concatenate([block[...] for block in blocks], axis=0)
    query = query_ref[:, start : start + 256]
    gate = jnp.dot(renorm[:, :320], query, preferred_element_type=F32)
    upper = jnp.dot(renorm[:, 320:640], query, preferred_element_type=F32)
    hidden = (gate * jax.nn.sigmoid(gate) * upper).astype(BF16)
    output = lax.dot_general(hidden, renorm[:, 640:], BY_TOKEN, preferred_element_type=F32)
    scaled = output * lax.rsqrt(jnp.mean(output * output, axis=-1, keepdims=True) + 1e-05)
    answer = scaled.astype(BF16)
    at = 0
    for out in outs:
        n = out.shape[0]
        out[:, :320] = answer[at : at + n]
        out[:, 320:] = answer[at + n : at + 2 * n]
        at += 2 * n


PLANE = [(0, 0, 64), (1, 0, 64), (2, 0, 64), (3, 0, 32), (4, 0, 32)]
OTHERS = [(0, 0, 32), (2, 0, 16), (4, 0, 16), (3, 0, 16), (4, 16, 32), (6, 0, 32)]
OTHERS += [(1, 0, 32), (2, 16, 32), (5, 0, 16), (3, 16, 32), (5, 16, 32), (7, 0, 32)]


def gather(tokens, work):
    near_tile, far_tile = to_near_x(tokens), to_far_x(tokens)
    z1, z2 = to_near_z(tokens[:32]), to_far_z(tokens[32:])
    near_first, far_second, first, second, both = call(
        split_kernel, [like((32, 5120))] * 5, near_tile, far_tile, z1, z2, after=work
    )
    opposite_first, opposite_second = to_far_x(near_first), to_near_x(far_second)
    z3, z4 = to_near_z(first), to_far_z(second)
    near_both, far_both = to_near_x(both), to_far_x(both)
    z5, z6 = to_near_z(opposite_first), to_far_z(opposite_second)
    return (
        [tokens, near_tile, far_tile, opposite_first, opposite_second],
        [z1, z2, near_both, far_both, z3, z4, z5, z6],
    )


OWN_HALF, OTHER_HALF, Y, BLOCK, SAME, OTHER, SLOT = 0, 1, 2, 3, 4, 8, 12


def table():
    lines = np.zeros((256, 32), np.int32)
    for i in range(256):
        _, y, core, z_lo, x = place(i)
        order = [x, near(x), far(x), (x + 2) % 4]
        lines[i, :4] = core * 320, 320 - core * 320, y, core * 320 + y * 80
        lines[i, SAME : SAME + 4] = [z_lo * 4 + t for t in order]
        lines[i, OTHER : OTHER + 4] = [(1 - z_lo) * 4 + t for t in order]
        lines[i, SLOT : SLOT + 8] = [order.index(h % 4) * 2 + (h // 4 != z_lo) for h in range(8)]
    return lines


def weights_kernel(my, rate, mask, weight, sent):
    for i in range(4):
        same = mask[pl.ds(my[SAME + i], 1), :].astype(F32) * rate[0]
        other = mask[pl.ds(my[OTHER + i], 1), :].astype(F32) * rate[0]
        weight[:, i * 64 : (i + 1) * 64] = same
        weight[:, 256 + i * 32 : 288 + i * 32] = other[:, :32]
        sent[:, i * 32 : (i + 1) * 32] = other[:, 32:]


def pieces_kernel(plane, from_near, from_far, *outs):
    for i, out in enumerate(outs):
        run = slice(i // 2 * 320, i // 2 * 320 + 320)
        half = slice(i % 2 * 32, i % 2 * 32 + 32)
        out[:, :320] = plane[i % 2 * 64 : i % 2 * 64 + 64, run]
        out[:32, 320:] = from_near[half, run]
        out[32:, 320:] = from_far[half, run]


def place_kernel(my, a, b, c, d, out, slots):
    for i, piece in enumerate((a, b, c, d)):
        slots[2 * i] = piece[:, :320]
        slots[2 * i + 1] = piece[:, 320:]
    for head in range(8):
        out[:, head * 320 : (head + 1) * 320] = slots[my[SLOT + head]]


def send_back(my, plane, for_near, for_far):
    pieces = call(
        pieces_kernel, [like((64, 640))] * 4, plane, to_near_z(for_near), to_far_z(for_far)
    )
    opposite = to_opposite_x(pieces[3])
    pieces = pieces[0], to_near_x(pieces[1]), to_far_x(pieces[2]), opposite
    return call(
        place_kernel,
        like((64, 2560)),
        my,
        *pieces,
        scalars=1,
        scratch=[pltpu.VMEM((8, 64, 320), BF16)],
    )


def body(tokens, w_qkv, scale_exp, gate_mask, rate, fast_gate, fast_up, fast_down):
    at = lax.axis_index("seq") * 8 + lax.axis_index("head")
    my = lax.dynamic_slice_in_dim(jnp.asarray(table()), at, 1, axis=0).reshape(32)
    tokens, my = lax.optimization_barrier((tokens, my))
    factor = jnp.exp2(scale_exp.astype(F32)).astype(BF16)[:, :, 0]
    factor = jnp.repeat(factor, w_qkv.shape[1] // factor.shape[1], axis=1)[:, None, :]
    w_t = jnp.transpose(w_qkv, (0, 2, 1))
    weight, sent = call(
        weights_kernel,
        [like((1, 384), F32), like((1, 128), F32)],
        my,
        rate,
        gate_mask.reshape(8, 64),
        scalars=2,
    )
    moved = permute(sent, lambda h, y, c, l, x: (h - 1 if l else h + 1, y, c, l, x))
    old_t = [w[0].T for w in (fast_gate, fast_up, fast_down)]
    weff = load(w_t, factor, 1, 2, after=(weight, *old_t))
    plane, others = gather(tokens, (weff,))
    kv1 = project(plane, PLANE, weff, after=others[2:6])
    kv2 = project(others, OTHERS, weff, after=(kv1,))

    grads = (my, kv1, kv2, weight, moved, *old_t)
    sent = call(
        functools.partial(grads_kernel, OTHER_HALF), like((320, 960)), *grads, scalars=1
    )
    got = to_core(sent)
    own = call(
        functools.partial(grads_kernel, OWN_HALF),
        like((320, 960), F32),
        *grads,
        scalars=1,
        after=(sent,),
    )
    to1, to2, to3, mine = call(
        halves_kernel, [like((80, 960))] * 3 + [like((80, 960), F32)], my, own, got, scalars=1
    )
    got = to_y(to2, 2), to_y(to1, 1), to_y(to3, 3)
    weff_q = load(w_t, factor, 0, 1, after=(to1,))
    parts = [like((80, 960), F32), like((40, 960)), like((40, 960))]
    mine, upper, lower = call(sum_kernel, parts, mine, *got, after=(weff_q,))

    got = to_near_h(upper), to_far_h(lower)
    cuts = PLANE + [(len(plane) + i, lo, hi) for i, lo, hi in OTHERS]
    query = project(plane + others, cuts, weff_q, after=(upper,))
    mine, upper, lower = call(pair_kernel, parts, mine, *got, after=(query,))
    got = to_far_h(upper), to_near_h(lower)
    block = call(renorm_kernel, like((80, 960)), my, mine, *got, *old_t, scalars=1)
    column = [block, to_y(block, 1), to_y(block, 3), to_y(block, 2)]
    blocks = column + [to_core(b) for b in column]

    for_near, for_far = call(
        functools.partial(respond_kernel, 256), [like((64, 640))] * 2, query, *blocks
    )
    (plane,) = call(
        functools.partial(respond_kernel, 0),
        [like((128, 640))],
        query,
        *blocks,
        after=(for_near,),
    )
    return send_back(my, plane, for_near, for_far)


def solution(mesh):
    in_specs = (
        P(("seq", "head"), None),
        P(None, None, "head"),
        P(None, None, "head"),
        P("seq", "head"),
        P("head"),
        P("head", None, None),
        P("head", None, None),
        P("head", None, None),
    )
    out_specs = P(("seq", "head"), None)
    return jax.shard_map(body, mesh=mesh, in_specs=in_specs, out_specs=out_specs, check_vma=False)
```

```python
import functools

import jax
import jax.numpy as jnp
import numpy as np
from jax import lax
from jax.experimental import pallas as pl
from jax.experimental.pallas import tpu as pltpu
from jax.sharding import PartitionSpec as P

AXES = ("seq", "head")
BF16 = jnp.bfloat16
F32 = jnp.float32


def place(i):
    seq, head = divmod(i, 8)
    return seq // 8, (seq // 2) % 4, seq % 2, head // 4, head % 4


def permute(value, move):
    pairs = []
    for i in range(256):
        z_hi, y, core, z_lo, x = move(*place(i))
        pairs.append((i, ((z_hi % 4) * 8 + (y % 4) * 2 + core) * 8 + z_lo * 4 + x % 4))
    return lax.ppermute(value, AXES, pairs)


def to_core(value):
    return permute(value, lambda h, y, c, l, x: (h, y, 1 - c, l, x))


def to_y(value, d):
    return permute(value, lambda h, y, c, l, x: (h, y + d, c, l, x))


def to_near_h(value):
    return permute(value, lambda h, y, c, l, x: (near(h), y, c, l, x))


def to_far_h(value):
    return permute(value, lambda h, y, c, l, x: (far(h), y, c, l, x))


def near(x):
    return x ^ 1


def far(x):
    return (x + 1) % 4 if x % 2 else (x - 1) % 4


def to_near_x(value):
    return permute(value, lambda h, y, c, l, x: (h, y, c, l, near(x)))


def to_far_x(value):
    return permute(value, lambda h, y, c, l, x: (h, y, c, l, far(x)))


def to_opposite_x(value):
    return permute(value, lambda h, y, c, l, x: (h, y, c, l, x + 2))


def to_near_z(value):
    return permute(value, lambda h, y, c, l, x: (h, y, c, 1 - l, x))


def to_far_z(value):
    return permute(value, lambda h, y, c, l, x: (h + 1 if l else h - 1, y, c, 1 - l, x))


VMEM = pl.BlockSpec(memory_space=pltpu.VMEM)
SMEM = pl.BlockSpec(memory_space=pltpu.SMEM)
SMALL = pl.CostEstimate(flops=1000, bytes_accessed=1000, transcendentals=0)
PARAMS = pltpu.CompilerParams(vmem_limit_bytes=20 * 1024 * 1024)
BY_ROW = (((1,), (1,)), ((), ()))
BY_TOKEN = (((0,), (0,)), ((), ()))


def like(shape, dtype=BF16):
    return jax.ShapeDtypeStruct(shape, dtype)


def call(kernel, out_shape, *args, scalars=0, after=(), scratch=()):
    n, skip = len(args), len(args) + len(after)

    def run(*refs):
        kernel(*refs[:n], *refs[skip:])

    return pl.pallas_call(
        run,
        out_shape=out_shape,
        in_specs=[SMEM] * scalars + [VMEM] * (n - scalars) + [VMEM] * len(after),
        out_specs=jax.tree.map(lambda _: VMEM, out_shape),
        scratch_shapes=list(scratch),
        compiler_params=PARAMS,
        cost_estimate=SMALL,
    )(*args, *after)


def split_kernel(near_tile, far_tile, z1, z2, near_first, far_second, first, second, both):
    near_first[...] = near_tile[:32, :]
    far_second[...] = far_tile[32:, :]
    first[:16, :] = near_tile[16:32, :]
    first[16:, :] = far_tile[16:32, :]
    second[:16, :] = near_tile[48:, :]
    second[16:, :] = far_tile[48:, :]
    both[:16, :] = z1[:16, :]
    both[16:, :] = z2[:16, :]


def load_kernel(first, w_hbm, f_ref, out, sems):
    copies = []
    for c in range(out.shape[0]):
        for i in range(4):
            at = pl.ds(i * 80, 80)
            source, target = w_hbm.at[first + c, at, :], out.at[c, at, :]
            copies.append((c, at, pltpu.make_async_copy(source, target, sems.at[c * 4 + i])))
    for _, _, copy in copies:
        copy.start()
    for c, at, copy in copies:
        copy.wait()
        out[c, at, :] = out[c, at, :] * f_ref[first + c]


def load(w_t, factor, first, count, after=()):
    def run(*refs):
        load_kernel(first, *refs[:2], *refs[-2:])

    return pl.pallas_call(
        run,
        out_shape=like((count, *w_t.shape[1:])),
        in_specs=[pl.BlockSpec(memory_space=pl.ANY), VMEM] + [VMEM] * len(after),
        out_specs=VMEM,
        scratch_shapes=[pltpu.SemaphoreType.DMA((count * 4,))],
        compiler_params=pltpu.CompilerParams(vmem_limit_bytes=44 * 1024 * 1024),
        cost_estimate=SMALL,
    )(w_t, factor, *after)


def project_kernel(cuts, *refs):
    tiles, (w_ref, out) = refs[:-2], refs[-2:]
    tile = jnp.concatenate([tiles[i][lo:hi, :] for i, lo, hi in cuts], axis=0)
    for c in range(w_ref.shape[0]):
        part = lax.dot_general(w_ref[c], tile, BY_ROW, preferred_element_type=F32)
        out[c * 320 : (c + 1) * 320, :] = part.astype(BF16)


def project(tiles, cuts, weff, after=()):
    shape = (weff.shape[0] * weff.shape[1], sum(hi - lo for _, lo, hi in cuts))
    return call(functools.partial(project_kernel, cuts), like(shape), *tiles, weff, after=after)


def grads_kernel(which, my, kv1, kv2, weight, moved, gate_t, up_t, down_t, out):
    half = pl.ds(pl.multiple_of(my[which], 16), 320)
    weight = jnp.concatenate([weight[...], moved[...]], axis=1)
    keys = jnp.concatenate([kv1[:320, :], kv2[:320, :]], axis=1)
    values = jnp.concatenate([kv1[320:, :], kv2[320:, :]], axis=1)
    gate = jnp.dot(gate_t[half, :], keys, preferred_element_type=F32)
    upper = jnp.dot(up_t[half, :], keys, preferred_element_type=F32)
    sigma = jax.nn.sigmoid(gate)
    active = gate * sigma
    hidden = (active * upper).astype(BF16)
    weighted = (weight * values.astype(F32)).astype(BF16)
    d_hidden = jnp.dot(down_t[half, :], weighted, preferred_element_type=F32)
    d_gate = (d_hidden * upper * sigma * (1.0 + gate * (1.0 - sigma))).astype(BF16)
    d_upper = (d_hidden * active).astype(BF16)
    pairs = ((d_gate, keys), (d_upper, keys), (hidden, weighted))
    for i, (left, right) in enumerate(pairs):
        grad = lax.dot_general(left, right, BY_ROW, preferred_element_type=F32)
        out[:, i * 320 : (i + 1) * 320] = grad.astype(out.dtype)


def halves_kernel(my, own, got, to1, to2, to3, mine):
    for d, out in ((1, to1), (2, to2), (3, to3), (0, mine)):
        at = pl.ds(pl.multiple_of(lax.rem(my[Y] + d, 4) * 80, 16), 80)
        out[...] = (own[at, :] + got[at, :].astype(F32)).astype(out.dtype)


def sum_kernel(mine, a, b, c, total, upper, lower):
    result = mine[...] + a[...].astype(F32) + b[...].astype(F32) + c[...].astype(F32)
    total[...] = result
    upper[...] = result[:40].astype(BF16)
    lower[...] = result[40:].astype(BF16)


def pair_kernel(mine, a, b, total, upper, lower):
    total[:40, :] = mine[:40, :] + a[...].astype(F32)
    total[40:, :] = mine[40:, :] + b[...].astype(F32)
    upper[...] = total[:40, :].astype(BF16)
    lower[...] = total[40:, :].astype(BF16)


def renorm_kernel(my, mine, a, b, gate_t, up_t, down_t, out):
    got = jnp.concatenate([a[...].astype(F32), b[...].astype(F32)], axis=0)
    total = mine[...] + got
    mine_rows = pl.ds(pl.multiple_of(my[BLOCK], 16), 80)
    for i, old in enumerate((gate_t, up_t, down_t)):
        at = slice(i * 320, (i + 1) * 320)
        before = old[mine_rows, :].astype(F32)
        fresh = before + total[:, at]
        old_norm = jnp.sqrt(jnp.sum(before * before, axis=1, keepdims=True))
        new_sq = jnp.sum(fresh * fresh, axis=1, keepdims=True)
        out[:, at] = (fresh * (old_norm / jnp.sqrt(new_sq + 1e-06))).astype(BF16)


def respond_kernel(start, query_ref, *refs):
    blocks, outs = refs[:8], refs[8:]
    renorm = jnp.concatenate([block[...] for block in blocks], axis=0)
    query = query_ref[:, start : start + 256]
    gate = jnp.dot(renorm[:, :320], query, preferred_element_type=F32)
    upper = jnp.dot(renorm[:, 320:640], query, preferred_element_type=F32)
    hidden = (gate * jax.nn.sigmoid(gate) * upper).astype(BF16)
    output = lax.dot_general(hidden, renorm[:, 640:], BY_TOKEN, preferred_element_type=F32)
    scaled = output * lax.rsqrt(jnp.mean(output * output, axis=-1, keepdims=True) + 1e-05)
    answer = scaled.astype(BF16)
    at = 0
    for out in outs:
        n = out.shape[0]
        out[:, :320] = answer[at : at + n]
        out[:, 320:] = answer[at + n : at + 2 * n]
        at += 2 * n


PLANE = [(0, 0, 64), (1, 0, 64), (2, 0, 64), (3, 0, 32), (4, 0, 32)]
OTHERS = [(0, 0, 32), (2, 0, 16), (4, 0, 16), (3, 0, 16), (4, 16, 32), (6, 0, 32)]
OTHERS += [(1, 0, 32), (2, 16, 32), (5, 0, 16), (3, 16, 32), (5, 16, 32), (7, 0, 32)]


def gather(tokens, same_tokens, work):
    near_tile, far_tile = to_near_x(tokens), to_far_x(tokens)
    z1, z2 = to_near_z(same_tokens[:32]), to_far_z(same_tokens[32:])
    near_first, far_second, first, second, both = call(
        split_kernel, [like((32, 5120))] * 5, near_tile, far_tile, z1, z2, after=work
    )
    opposite_first, opposite_second = to_far_x(near_first), to_near_x(far_second)
    z3, z4 = to_near_z(first), to_far_z(second)
    near_both, far_both = to_near_x(both), to_far_x(both)
    z5, z6 = to_near_z(opposite_first), to_far_z(opposite_second)
    return (
        [tokens, near_tile, far_tile, opposite_first, opposite_second],
        [z1, z2, near_both, far_both, z3, z4, z5, z6],
    )


OWN_HALF, OTHER_HALF, Y, BLOCK, SAME, OTHER, SLOT = 0, 1, 2, 3, 4, 8, 12


def table():
    lines = np.zeros((256, 32), np.int32)
    for i in range(256):
        _, y, core, z_lo, x = place(i)
        order = [x, near(x), far(x), (x + 2) % 4]
        lines[i, :4] = core * 320, 320 - core * 320, y, core * 320 + y * 80
        lines[i, SAME : SAME + 4] = [z_lo * 4 + t for t in order]
        lines[i, OTHER : OTHER + 4] = [(1 - z_lo) * 4 + t for t in order]
        lines[i, SLOT : SLOT + 8] = [order.index(h % 4) * 2 + (h // 4 != z_lo) for h in range(8)]
    return lines


def weights_kernel(my, rate, mask, weight, sent):
    for i in range(4):
        same = mask[pl.ds(my[SAME + i], 1), :].astype(F32) * rate[0]
        other = mask[pl.ds(my[OTHER + i], 1), :].astype(F32) * rate[0]
        weight[:, i * 64 : (i + 1) * 64] = same
        weight[:, 256 + i * 32 : 288 + i * 32] = other[:, :32]
        sent[:, i * 32 : (i + 1) * 32] = other[:, 32:]


def pieces_kernel(plane, from_near, from_far, *outs):
    for i, out in enumerate(outs):
        run = slice(i // 2 * 320, i // 2 * 320 + 320)
        half = slice(i % 2 * 32, i % 2 * 32 + 32)
        out[:, :320] = plane[i % 2 * 64 : i % 2 * 64 + 64, run]
        out[:32, 320:] = from_near[half, run]
        out[32:, 320:] = from_far[half, run]


def place_kernel(my, a, b, c, d, out, slots):
    for i, piece in enumerate((a, b, c, d)):
        slots[2 * i] = piece[:, :320]
        slots[2 * i + 1] = piece[:, 320:]
    for head in range(8):
        out[:, head * 320 : (head + 1) * 320] = slots[my[SLOT + head]]


def send_back(my, plane, for_near, for_far):
    pieces = call(
        pieces_kernel, [like((64, 640))] * 4, plane, to_near_z(for_near), to_far_z(for_far)
    )
    opposite = to_opposite_x(pieces[3])
    pieces = pieces[0], to_near_x(pieces[1]), to_far_x(pieces[2]), opposite
    return call(
        place_kernel,
        like((64, 2560)),
        my,
        *pieces,
        scalars=1,
        scratch=[pltpu.VMEM((8, 64, 320), BF16)],
    )


def body(tokens, w_qkv, scale_exp, gate_mask, rate, fast_gate, fast_up, fast_down):
    at = lax.axis_index("seq") * 8 + lax.axis_index("head")
    my = lax.dynamic_slice_in_dim(jnp.asarray(table()), at, 1, axis=0).reshape(32)
    same_tokens, my = lax.optimization_barrier((tokens, my))
    factor = jnp.exp2(scale_exp.astype(F32)).astype(BF16)[:, :, 0]
    factor = jnp.repeat(factor, w_qkv.shape[1] // factor.shape[1], axis=1)[:, None, :]
    w_t = jnp.transpose(w_qkv, (0, 2, 1))
    weight, sent = call(
        weights_kernel,
        [like((1, 384), F32), like((1, 128), F32)],
        my,
        rate,
        gate_mask.reshape(8, 64),
        scalars=2,
    )
    moved = permute(sent, lambda h, y, c, l, x: (h - 1 if l else h + 1, y, c, l, x))
    old_t = [w[0].T for w in (fast_gate, fast_up, fast_down)]
    weff = load(w_t, factor, 1, 2, after=(weight, *old_t))
    plane, others = gather(tokens, same_tokens, (weff,))
    kv1 = project(plane, PLANE, weff, after=others[2:6])
    kv2 = project(others, OTHERS, weff, after=(kv1,))

    grads = (my, kv1, kv2, weight, moved, *old_t)
    sent = call(
        functools.partial(grads_kernel, OTHER_HALF), like((320, 960)), *grads, scalars=1
    )
    got = to_core(sent)
    own = call(
        functools.partial(grads_kernel, OWN_HALF),
        like((320, 960), F32),
        *grads,
        scalars=1,
        after=(sent,),
    )
    to1, to2, to3, mine = call(
        halves_kernel, [like((80, 960))] * 3 + [like((80, 960), F32)], my, own, got, scalars=1
    )
    got = to_y(to2, 2), to_y(to1, 1), to_y(to3, 3)
    weff_q = load(w_t, factor, 0, 1, after=(to1,))
    parts = [like((80, 960), F32), like((40, 960)), like((40, 960))]
    mine, upper, lower = call(sum_kernel, parts, mine, *got, after=(weff_q,))

    got = to_near_h(upper), to_far_h(lower)
    cuts = PLANE + [(len(plane) + i, lo, hi) for i, lo, hi in OTHERS]
    query = project(plane + others, cuts, weff_q, after=(upper,))
    mine, upper, lower = call(pair_kernel, parts, mine, *got, after=(query,))
    got = to_far_h(upper), to_near_h(lower)
    block = call(renorm_kernel, like((80, 960)), my, mine, *got, *old_t, scalars=1)
    column = [block, to_y(block, 1), to_y(block, 3), to_y(block, 2)]
    blocks = column + [to_core(b) for b in column]

    for_near, for_far = call(
        functools.partial(respond_kernel, 256), [like((64, 640))] * 2, query, *blocks
    )
    (plane,) = call(
        functools.partial(respond_kernel, 0),
        [like((128, 640))],
        query,
        *blocks,
        after=(for_near,),
    )
    return send_back(my, plane, for_near, for_far)


def solution(mesh):
    in_specs = (
        P(("seq", "head"), None),
        P(None, None, "head"),
        P(None, None, "head"),
        P("seq", "head"),
        P("head"),
        P("head", None, None),
        P("head", None, None),
        P("head", None, None),
    )
    out_specs = P(("seq", "head"), None)
    return jax.shard_map(body, mesh=mesh, in_specs=in_specs, out_specs=out_specs, check_vma=False)
```

```python
import functools

import jax
import jax.numpy as jnp
import numpy as np
from jax import lax
from jax.experimental import pallas as pl
from jax.experimental.pallas import tpu as pltpu
from jax.sharding import PartitionSpec as P

AXES = ("seq", "head")
BF16 = jnp.bfloat16
F32 = jnp.float32


def place(i):
    seq, head = divmod(i, 8)
    return seq // 8, (seq // 2) % 4, seq % 2, head // 4, head % 4


def permute(value, move):
    pairs = []
    for i in range(256):
        z_hi, y, core, z_lo, x = move(*place(i))
        pairs.append((i, ((z_hi % 4) * 8 + (y % 4) * 2 + core) * 8 + z_lo * 4 + x % 4))
    return lax.ppermute(value, AXES, pairs)


def to_core(value):
    return permute(value, lambda h, y, c, l, x: (h, y, 1 - c, l, x))


def to_y(value, d):
    return permute(value, lambda h, y, c, l, x: (h, y + d, c, l, x))


def to_near_h(value):
    return permute(value, lambda h, y, c, l, x: (near(h), y, c, l, x))


def to_far_h(value):
    return permute(value, lambda h, y, c, l, x: (far(h), y, c, l, x))


def near(x):
    return x ^ 1


def far(x):
    return (x + 1) % 4 if x % 2 else (x - 1) % 4


def to_near_x(value):
    return permute(value, lambda h, y, c, l, x: (h, y, c, l, near(x)))


def to_far_x(value):
    return permute(value, lambda h, y, c, l, x: (h, y, c, l, far(x)))


def to_opposite_x(value):
    return permute(value, lambda h, y, c, l, x: (h, y, c, l, x + 2))


def to_near_z(value):
    return permute(value, lambda h, y, c, l, x: (h, y, c, 1 - l, x))


def to_far_z(value):
    return permute(value, lambda h, y, c, l, x: (h + 1 if l else h - 1, y, c, 1 - l, x))


VMEM = pl.BlockSpec(memory_space=pltpu.VMEM)
SMEM = pl.BlockSpec(memory_space=pltpu.SMEM)
SMALL = pl.CostEstimate(flops=1000, bytes_accessed=1000, transcendentals=0)
PARAMS = pltpu.CompilerParams(vmem_limit_bytes=20 * 1024 * 1024)
BY_ROW = (((1,), (1,)), ((), ()))
BY_TOKEN = (((0,), (0,)), ((), ()))


def like(shape, dtype=BF16):
    return jax.ShapeDtypeStruct(shape, dtype)


def call(kernel, out_shape, *args, scalars=0, after=(), scratch=()):
    n, skip = len(args), len(args) + len(after)

    def run(*refs):
        kernel(*refs[:n], *refs[skip:])

    return pl.pallas_call(
        run,
        out_shape=out_shape,
        in_specs=[SMEM] * scalars + [VMEM] * (n - scalars) + [VMEM] * len(after),
        out_specs=jax.tree.map(lambda _: VMEM, out_shape),
        scratch_shapes=list(scratch),
        compiler_params=PARAMS,
        cost_estimate=SMALL,
    )(*args, *after)


def split_kernel(near_tile, far_tile, z1, z2, near_first, far_second, first, second, both):
    near_first[...] = near_tile[:32, :]
    far_second[...] = far_tile[32:, :]
    first[:16, :] = near_tile[16:32, :]
    first[16:, :] = far_tile[16:32, :]
    second[:16, :] = near_tile[48:, :]
    second[16:, :] = far_tile[48:, :]
    both[:16, :] = z1[:16, :]
    both[16:, :] = z2[:16, :]


def load_kernel(first, w_hbm, f_ref, out, sems):
    copies = []
    for c in range(out.shape[0]):
        for i in range(4):
            at = pl.ds(i * 80, 80)
            source, target = w_hbm.at[first + c, at, :], out.at[c, at, :]
            copies.append((c, at, pltpu.make_async_copy(source, target, sems.at[c * 4 + i])))
    for _, _, copy in copies:
        copy.start()
    for c, at, copy in copies:
        copy.wait()
        out[c, at, :] = out[c, at, :] * f_ref[first + c]


def load(w_t, factor, first, count, after=()):
    def run(*refs):
        load_kernel(first, *refs[:2], *refs[-2:])

    return pl.pallas_call(
        run,
        out_shape=like((count, *w_t.shape[1:])),
        in_specs=[pl.BlockSpec(memory_space=pl.ANY), VMEM] + [VMEM] * len(after),
        out_specs=VMEM,
        scratch_shapes=[pltpu.SemaphoreType.DMA((count * 4,))],
        compiler_params=pltpu.CompilerParams(vmem_limit_bytes=44 * 1024 * 1024),
        cost_estimate=SMALL,
    )(w_t, factor, *after)


def project_kernel(cuts, *refs):
    tiles, (w_ref, out) = refs[:-2], refs[-2:]
    tile = jnp.concatenate([tiles[i][lo:hi, :] for i, lo, hi in cuts], axis=0)
    for c in range(w_ref.shape[0]):
        part = lax.dot_general(w_ref[c], tile, BY_ROW, preferred_element_type=F32)
        out[c * 320 : (c + 1) * 320, :] = part.astype(BF16)


def project(tiles, cuts, weff, after=()):
    shape = (weff.shape[0] * weff.shape[1], sum(hi - lo for _, lo, hi in cuts))
    return call(functools.partial(project_kernel, cuts), like(shape), *tiles, weff, after=after)


def grads_kernel(which, planes, my, kv, weight, gate_t, up_t, down_t, *refs):
    half = pl.ds(pl.multiple_of(my[which], 16), 320)
    out = refs[-1]
    keys, values = kv[:320, :], kv[320:, :]
    if planes:
        weight = weight[:, :256]
    else:
        weight = jnp.concatenate([weight[:, 256:], refs[0][...]], axis=1)
    gate = jnp.dot(gate_t[half, :], keys, preferred_element_type=F32)
    upper = jnp.dot(up_t[half, :], keys, preferred_element_type=F32)
    sigma = jax.nn.sigmoid(gate)
    active = gate * sigma
    hidden = (active * upper).astype(BF16)
    weighted = (weight * values.astype(F32)).astype(BF16)
    d_hidden = jnp.dot(down_t[half, :], weighted, preferred_element_type=F32)
    d_gate = (d_hidden * upper * sigma * (1.0 + gate * (1.0 - sigma))).astype(BF16)
    d_upper = (d_hidden * active).astype(BF16)
    pairs = ((d_gate, keys), (d_upper, keys), (hidden, weighted))
    for i, (left, right) in enumerate(pairs):
        grad = lax.dot_general(left, right, BY_ROW, preferred_element_type=F32)
        at = slice(i * 320, (i + 1) * 320)
        if not planes:
            grad += refs[1][:, at]
        out[:, at] = grad.astype(out.dtype)


def halves_kernel(my, own, got, to1, to2, to3, mine):
    for d, out in ((1, to1), (2, to2), (3, to3), (0, mine)):
        at = pl.ds(pl.multiple_of(lax.rem(my[Y] + d, 4) * 80, 16), 80)
        out[...] = (own[at, :] + got[at, :].astype(F32)).astype(out.dtype)


def sum_kernel(mine, a, b, c, total, upper, lower):
    result = mine[...] + a[...].astype(F32) + b[...].astype(F32) + c[...].astype(F32)
    total[...] = result
    upper[...] = result[:40].astype(BF16)
    lower[...] = result[40:].astype(BF16)


def pair_kernel(mine, a, b, total, upper, lower):
    total[:40, :] = mine[:40, :] + a[...].astype(F32)
    total[40:, :] = mine[40:, :] + b[...].astype(F32)
    upper[...] = total[:40, :].astype(BF16)
    lower[...] = total[40:, :].astype(BF16)


def renorm_kernel(my, mine, a, b, gate_t, up_t, down_t, out):
    got = jnp.concatenate([a[...].astype(F32), b[...].astype(F32)], axis=0)
    total = mine[...] + got
    mine_rows = pl.ds(pl.multiple_of(my[BLOCK], 16), 80)
    for i, old in enumerate((gate_t, up_t, down_t)):
        at = slice(i * 320, (i + 1) * 320)
        before = old[mine_rows, :].astype(F32)
        fresh = before + total[:, at]
        old_norm = jnp.sqrt(jnp.sum(before * before, axis=1, keepdims=True))
        new_sq = jnp.sum(fresh * fresh, axis=1, keepdims=True)
        out[:, at] = (fresh * (old_norm / jnp.sqrt(new_sq + 1e-06))).astype(BF16)


def respond_kernel(start, query_ref, *refs):
    blocks, outs = refs[:8], refs[8:]
    renorm = jnp.concatenate([block[...] for block in blocks], axis=0)
    query = query_ref[:, start : start + 256]
    gate = jnp.dot(renorm[:, :320], query, preferred_element_type=F32)
    upper = jnp.dot(renorm[:, 320:640], query, preferred_element_type=F32)
    hidden = (gate * jax.nn.sigmoid(gate) * upper).astype(BF16)
    output = lax.dot_general(hidden, renorm[:, 640:], BY_TOKEN, preferred_element_type=F32)
    scaled = output * lax.rsqrt(jnp.mean(output * output, axis=-1, keepdims=True) + 1e-05)
    answer = scaled.astype(BF16)
    at = 0
    for out in outs:
        n = out.shape[0]
        out[:, :320] = answer[at : at + n]
        out[:, 320:] = answer[at + n : at + 2 * n]
        at += 2 * n


PLANE = [(0, 0, 64), (1, 0, 64), (2, 0, 64), (3, 0, 32), (4, 0, 32)]
OTHERS = [(0, 0, 32), (2, 0, 16), (4, 0, 16), (3, 0, 16), (4, 16, 32), (6, 0, 32)]
OTHERS += [(1, 0, 32), (2, 16, 32), (5, 0, 16), (3, 16, 32), (5, 16, 32), (7, 0, 32)]


def gather(tokens, same_tokens, work):
    near_tile, far_tile = to_near_x(tokens), to_far_x(tokens)
    z1, z2 = to_near_z(same_tokens[:32]), to_far_z(same_tokens[32:])
    near_first, far_second, first, second, both = call(
        split_kernel, [like((32, 5120))] * 5, near_tile, far_tile, z1, z2, after=work
    )
    opposite_first, opposite_second = to_far_x(near_first), to_near_x(far_second)
    z3, z4 = to_near_z(first), to_far_z(second)
    near_both, far_both = to_near_x(both), to_far_x(both)
    z5, z6 = to_near_z(opposite_first), to_far_z(opposite_second)
    return (
        [tokens, near_tile, far_tile, opposite_first, opposite_second],
        [z1, z2, near_both, far_both, z3, z4, z5, z6],
    )


OWN_HALF, OTHER_HALF, Y, BLOCK, SAME, OTHER, SLOT = 0, 1, 2, 3, 4, 8, 12


def table():
    lines = np.zeros((256, 32), np.int32)
    for i in range(256):
        _, y, core, z_lo, x = place(i)
        order = [x, near(x), far(x), (x + 2) % 4]
        lines[i, :4] = core * 320, 320 - core * 320, y, core * 320 + y * 80
        lines[i, SAME : SAME + 4] = [z_lo * 4 + t for t in order]
        lines[i, OTHER : OTHER + 4] = [(1 - z_lo) * 4 + t for t in order]
        lines[i, SLOT : SLOT + 8] = [order.index(h % 4) * 2 + (h // 4 != z_lo) for h in range(8)]
    return lines


def weights_kernel(my, rate, mask, weight, sent):
    for i in range(4):
        same = mask[pl.ds(my[SAME + i], 1), :].astype(F32) * rate[0]
        other = mask[pl.ds(my[OTHER + i], 1), :].astype(F32) * rate[0]
        weight[:, i * 64 : (i + 1) * 64] = same
        weight[:, 256 + i * 32 : 288 + i * 32] = other[:, :32]
        sent[:, i * 32 : (i + 1) * 32] = other[:, 32:]


def pieces_kernel(plane, from_near, from_far, *outs):
    for i, out in enumerate(outs):
        run = slice(i // 2 * 320, i // 2 * 320 + 320)
        half = slice(i % 2 * 32, i % 2 * 32 + 32)
        out[:, :320] = plane[i % 2 * 64 : i % 2 * 64 + 64, run]
        out[:32, 320:] = from_near[half, run]
        out[32:, 320:] = from_far[half, run]


def place_kernel(my, a, b, c, d, out, slots):
    for i, piece in enumerate((a, b, c, d)):
        slots[2 * i] = piece[:, :320]
        slots[2 * i + 1] = piece[:, 320:]
    for head in range(8):
        out[:, head * 320 : (head + 1) * 320] = slots[my[SLOT + head]]


def send_back(my, plane, for_near, for_far):
    pieces = call(
        pieces_kernel, [like((64, 640))] * 4, plane, to_near_z(for_near), to_far_z(for_far)
    )
    opposite = to_opposite_x(pieces[3])
    pieces = pieces[0], to_near_x(pieces[1]), to_far_x(pieces[2]), opposite
    return call(
        place_kernel,
        like((64, 2560)),
        my,
        *pieces,
        scalars=1,
        scratch=[pltpu.VMEM((8, 64, 320), BF16)],
    )


def body(tokens, w_qkv, scale_exp, gate_mask, rate, fast_gate, fast_up, fast_down):
    at = lax.axis_index("seq") * 8 + lax.axis_index("head")
    my = lax.dynamic_slice_in_dim(jnp.asarray(table()), at, 1, axis=0).reshape(32)
    same_tokens, my = lax.optimization_barrier((tokens, my))
    factor = jnp.exp2(scale_exp.astype(F32)).astype(BF16)[:, :, 0]
    factor = jnp.repeat(factor, w_qkv.shape[1] // factor.shape[1], axis=1)[:, None, :]
    w_t = jnp.transpose(w_qkv, (0, 2, 1))
    weight, sent = call(
        weights_kernel,
        [like((1, 384), F32), like((1, 128), F32)],
        my,
        rate,
        gate_mask.reshape(8, 64),
        scalars=2,
    )
    moved = permute(sent, lambda h, y, c, l, x: (h - 1 if l else h + 1, y, c, l, x))
    old_t = [w[0].T for w in (fast_gate, fast_up, fast_down)]
    weff = load(w_t, factor, 1, 2, after=(weight, *old_t))
    plane, others = gather(tokens, same_tokens, (weff,))
    kv1 = project(plane, PLANE, weff, after=others[2:6])

    def grads(which, planes, *args, dtype=F32, after=()):
        kernel = functools.partial(grads_kernel, which, planes)
        args = (my, args[0], weight, *old_t, *args[1:])
        return call(kernel, like((320, 960), dtype), *args, scalars=1, after=after)

    base_other, base_own = grads(OTHER_HALF, True, kv1), grads(OWN_HALF, True, kv1)
    kv2 = project(others, OTHERS, weff, after=(kv1, base_other, base_own))
    sent = grads(OTHER_HALF, False, kv2, moved, base_other, dtype=BF16)
    got = to_core(sent)
    own = grads(OWN_HALF, False, kv2, moved, base_own, after=(sent,))
    to1, to2, to3, mine = call(
        halves_kernel, [like((80, 960))] * 3 + [like((80, 960), F32)], my, own, got, scalars=1
    )
    got = to_y(to2, 2), to_y(to1, 1), to_y(to3, 3)
    weff_q = load(w_t, factor, 0, 1, after=(to1,))
    parts = [like((80, 960), F32), like((40, 960)), like((40, 960))]
    mine, upper, lower = call(sum_kernel, parts, mine, *got, after=(weff_q,))

    got = to_near_h(upper), to_far_h(lower)
    cuts = PLANE + [(len(plane) + i, lo, hi) for i, lo, hi in OTHERS]
    query = project(plane + others, cuts, weff_q, after=(upper,))
    mine, upper, lower = call(pair_kernel, parts, mine, *got, after=(query,))
    got = to_far_h(upper), to_near_h(lower)
    block = call(renorm_kernel, like((80, 960)), my, mine, *got, *old_t, scalars=1)
    column = [block, to_y(block, 1), to_y(block, 3), to_y(block, 2)]
    blocks = column + [to_core(b) for b in column]

    for_near, for_far = call(
        functools.partial(respond_kernel, 256), [like((64, 640))] * 2, query, *blocks
    )
    (plane,) = call(
        functools.partial(respond_kernel, 0),
        [like((128, 640))],
        query,
        *blocks,
        after=(for_near,),
    )
    return send_back(my, plane, for_near, for_far)


def solution(mesh):
    in_specs = (
        P(("seq", "head"), None),
        P(None, None, "head"),
        P(None, None, "head"),
        P("seq", "head"),
        P("head"),
        P("head", None, None),
        P("head", None, None),
        P("head", None, None),
    )
    out_specs = P(("seq", "head"), None)
    return jax.shard_map(body, mesh=mesh, in_specs=in_specs, out_specs=out_specs, check_vma=False)
```
